256 devices in a mesh: section: 16 (over z, core), expert: 16 (over x, y).
Axes of the slice: x: 4, y: 4, z: 8, core: 2. Of those that a mesh axis runs over, the one named last changes fastest.
Arguments:
- tokens: bfloat16 [2048, 3072], P('expert'), may hold values from -6 to 6
- norm_gain: float32 [3072], replicated, may hold values from 0.1 to 1.9
- expert_ids: int32 [2048, 4], P('expert'), may hold values from 0 to 15, all different within a row; in each aligned block of 128 rows (0 to 127, 128 to 255, ...) at most 64 rows name the same one
- gates: float32 [2048, 4], P('expert'), may hold values from 0.1 to 1
- gate_proj: bfloat16 [16, 3072, 8192], P('expert', None, 'section'), may hold values from -0.109375 to 0.109375
- up_proj: bfloat16 [16, 3072, 8192], P('expert', None, 'section'), may hold values from -0.109375 to 0.109375
- down_proj: bfloat16 [16, 8192, 3072], P('expert', 'section'), may hold values from -0.0625 to 0.0625
Outputs:
- mixed: bfloat16 [2048, 3072], P('expert')
The draws below stay inside these ranges and needn't reach their ends.
Inputs may be any that keep to these rules, and one draw needn't show every extreme that they name: `expert_ids`: each token names 4 different experts; among the 128 tokens of one aligned block no expert is named more than 64 times, and in every draw some block names some expert exactly 64 times.
All inputs are finite; a program needn't handle non-finite values.
Results may differ from the reference program's by a relative error of at most 0.024.
Values may be sent and summed in bfloat16 or wider, within the bound.
A program may use at most 64 MiB of HBM per device.

```python
import math
import jax
import jax.numpy as jnp
import numpy as np
from jax import lax

D = 3072
FF = 8192
TOP = 4
TOK_DEV = 128
EXPERTS = 16
CAP = 64
TOKENS = 2048
N_SECTION = 16
N_EXPERT = 16


def block_levels(own_key, dims, shards, low, high):
    gain, own = 1.0, jax.random.fold_in(own_key, 6)
    for dim, blocks in shards:
        draws = jnp.exp(jax.random.uniform(jax.random.fold_in(own, dim), (blocks,), jnp.float32, low / len(shards), high / len(shards)))
        gain = gain * jnp.repeat(draws, dims[dim] // blocks).reshape([-1 if axis == dim else 1 for axis in range(len(dims))])
    return gain


def routed_block(own_key, own, number, rows, number_of, top, bound, lean):
    order = jax.random.permutation(own_key, number_of)
    crowded, common = load_shares(number_of, rows * top, bound, lean, True), load_shares(number_of, rows * top, bound, lean, False)
    places = jnp.arange(number_of)

    def named(sizes, offset_by):
        used = int((sizes > 0).sum())
        fixed = max(1, used // 4)
        shifted = fixed + (places - fixed + offset_by * (used - fixed)) % max(1, number_of - fixed)
        return jnp.zeros((number_of,), jnp.int32).at[order[jnp.where(places < fixed, places, shifted)]].set(jnp.asarray(sizes, jnp.int32))

    sizes = jnp.where(number % 4 == 0, named(crowded, number // 4), named(common, number - number // 4 - 1))
    mixed = jax.random.permutation(jax.random.fold_in(own, 3), number_of)
    donor, sink = mixed[0:number_of // 2 * 2:2], mixed[1:number_of // 2 * 2:2]
    margin = jnp.minimum(sizes[donor] - 1, bound - sizes[sink]) // 2
    margin = jnp.where((donor == order[0]) | (sink == order[0]) | (sizes[sink] == 0), 0, jnp.maximum(margin, 0))
    shifted = jax.random.randint(jax.random.fold_in(own, 4), (number_of // 2,), 0, 1 << 20) % (margin + 1)
    sizes = sizes.at[donor].add(-shifted).at[sink].add(shifted)
    members = jnp.searchsorted(jnp.cumsum(sizes), jnp.arange(rows * top), side="right").astype(jnp.int32)
    table = members.reshape(top, rows).T
    table = table[jax.random.permutation(jax.random.fold_in(own, 1), rows)]
    offset_by = jax.random.randint(jax.random.fold_in(own, 2), (rows, 1), 0, top)
    return jnp.take_along_axis(table, (jnp.arange(top)[None, :] + offset_by) % top, axis=1)


def load_shares(amount, total, limit, slope, full):
    loads = [(1 << 20) // math.isqrt(rank ** slope) + 1 for rank in range(1, amount + 1)]
    largest = limit if full else min(limit, max(-(-total // amount), total * loads[0] // sum(loads)))
    least = 1 if total - largest >= amount - 1 else 0
    counts, surplus = [largest] + [least] * (amount - 1), total - largest - least * (amount - 1)
    while surplus > 0:
        candidates = [i for i in range(1, amount) if counts[i] < largest] or [i for i in range(1, amount) if counts[i] < limit]
        pool, remaining = sum([loads[i] for i in candidates]), surplus
        for i in candidates:
            more = min(limit - counts[i], max(1, remaining * loads[i] // pool), surplus)
            counts[i] = counts[i] + more
            surplus = surplus - more
    return np.array(counts)


def scatter_about(own_key, shape, width, limit, cuts=(), held_as=jnp.bfloat16):
    result = width * jax.random.normal(own_key, shape, jnp.float32)
    if cuts:
        result = result * block_levels(own_key, shape, cuts, -0.22, 0.18)
    return jnp.clip(result, -limit, limit).astype(held_as)


def setup_inputs(seed: int = 0) -> dict:
    splits = jax.random.split(jax.random.key(seed), 8)
    tokens = scatter_about(splits[0], (TOKENS, D), 1.0, 6.0, ((0, 16),))
    norm_gain = jnp.clip(1.0 + 0.18 * jax.random.normal(splits[1], (D,), jnp.float32), 0.1, 1.9)
    expert_ids_keys = jax.random.split(jax.random.fold_in(splits[2], 1), TOKENS // TOK_DEV)
    expert_ids_turns = jax.random.permutation(jax.random.fold_in(splits[2], 3), TOKENS // TOK_DEV)
    expert_ids = jax.vmap(lambda own, number: routed_block(jax.random.fold_in(splits[2], 2), own, number, TOK_DEV, EXPERTS, TOP, CAP, 2))(expert_ids_keys, expert_ids_turns).reshape((TOKENS, TOP))
    gates = jnp.clip(jnp.exp(math.log(1.0) - 2.3025851 * jax.random.uniform(splits[3], (TOKENS, TOP), jnp.float32) ** block_levels(splits[3], (TOKENS, TOP), ((0, 16),), -0.2, 0.2)), 0.1, 1.0)
    gate_proj = scatter_about(splits[4], (EXPERTS, D, FF), D ** -0.5, 0.109375, ((0, 16), (2, 16)))
    up_proj = scatter_about(splits[5], (EXPERTS, D, FF), D ** -0.5, 0.109375, ((0, 16), (2, 16)))
    down_proj = scatter_about(splits[6], (EXPERTS, FF, D), FF ** -0.5, 0.0625, ((0, 16), (1, 16)))
    return {"tokens": tokens, "norm_gain": norm_gain, "expert_ids": expert_ids, "gates": gates, "gate_proj": gate_proj, "up_proj": up_proj, "down_proj": down_proj}


def reference(tokens, norm_gain, expert_ids, gates, gate_proj, up_proj, down_proj):
    device_count = N_EXPERT
    values = tokens.astype(jnp.float32)
    average = lax.optimization_barrier(jnp.mean(values, axis=-1, keepdims=True))
    centered = values - average
    variance = lax.optimization_barrier(jnp.mean(centered * centered, axis=-1, keepdims=True))
    normed = (centered * lax.rsqrt(variance + 1e-05) * norm_gain.astype(jnp.float32)).astype(jnp.bfloat16)
    choices = expert_ids.reshape(device_count, TOK_DEV * TOP).astype(jnp.int32)
    onehot = (choices[:, :, None] == jnp.arange(EXPERTS, dtype=jnp.int32)[None, None, :]).astype(jnp.int32)
    slot_index = lax.optimization_barrier(jnp.sum((jnp.cumsum(onehot, axis=1) - onehot) * onehot, axis=-1)).astype(jnp.int32)
    owner_block = jnp.broadcast_to(jnp.arange(device_count, dtype=jnp.int32)[:, None], choices.shape)
    spread = jnp.repeat(normed.reshape(device_count, TOK_DEV, D), TOP, axis=1)
    packed = jnp.zeros((EXPERTS, device_count, CAP, D), jnp.bfloat16).at[choices, owner_block, slot_index].set(spread)
    group = FF // N_SECTION

    def expert_block(operands):
        buffer, gate_weight, up_weight, down_weight = operands
        flattened = buffer.reshape(device_count * CAP, D)
        gate_value = jnp.dot(flattened, gate_weight, preferred_element_type=jnp.float32)
        up_value = jnp.dot(flattened, up_weight, preferred_element_type=jnp.float32)
        hidden = (jax.nn.silu(gate_value) * up_value).astype(jnp.bfloat16)

        def add_group(running, operand_pair):
            slice_hidden, slice_down = operand_pair
            term = jnp.dot(slice_hidden, slice_down, preferred_element_type=jnp.float32).astype(jnp.bfloat16)
            term = lax.optimization_barrier(term)
            return (running + term.astype(jnp.float32), None)
        pieces = (hidden.reshape(device_count * CAP, N_SECTION, group).transpose(1, 0, 2), down_weight.reshape(N_SECTION, group, D))
        running, _ = lax.scan(add_group, jnp.zeros((device_count * CAP, D), jnp.float32), pieces)
        return running.astype(jnp.bfloat16).reshape(device_count, CAP, D)
    results = lax.map(expert_block, (packed, gate_proj, up_proj, down_proj))
    picked = results[choices, owner_block, slot_index].astype(jnp.float32)
    weights = gates.reshape(device_count, TOK_DEV * TOP).astype(jnp.float32)
    mixed_rows = lax.optimization_barrier(jnp.sum((picked * weights[:, :, None]).reshape(device_count, TOK_DEV, TOP, D), axis=2))
    return mixed_rows.reshape(TOKENS, D).astype(jnp.bfloat16)
```

```python
import functools

import jax
import jax.numpy as jnp
from jax import lax
from jax.experimental import pallas as pl
from jax.experimental.pallas import tpu as pltpu
from jax.sharding import PartitionSpec as P

MESH = pl.DeviceIdType.MESH
BATCHES = 4
SLOTS = 16
NZ = 8
SIDE = 4
XY = [(dx, dy) for dx in range(SIDE) for dy in range(SIDE) if (dx, dy) != (0, 0)]
ORDER = (4, 3, 5, 2, 6, 1, 7, 0)
BF = jnp.bfloat16
F32 = jnp.float32


def kernel(
    tok, gain, ids, gates, wg_hbm, wu_hbm, wd_hbm, out,
    wg, wu, wd, normed, sel, chi, clo, packed, xin, gacc, uacc, part, sib,
    asend, arecv, bsend, brecv, ret_out, ret, acc, mixed,
    w_sem, xs, xr, fs, fr, ps, pr, as_, ar, bs, br, rs, rr, os_, or_, gs, gr,
):
    sec, me = lax.axis_index("section"), lax.axis_index("expert")
    z, c = sec // 2, sec % 2
    x, y = me // SIDE, me % SIDE
    experts = SIDE * SIDE
    half = normed.shape[2]
    width = wg.shape[2]
    chunk = wd.shape[2]
    rows = experts * SLOTS
    hrows = rows // 2
    sigma = 1 - 2 * c

    def zdev(dz, cc):
        return (lax.rem(z + dz + 2 * NZ, NZ) * 2 + cc, me)

    def xydev(dx, dy):
        return lax.rem(x + dx, SIDE) * SIDE + lax.rem(y + dy, SIDE)

    def rel(k):
        return lax.rem(k + 2 * NZ, NZ)

    sibling = (z * 2 + 1 - c, me)

    barrier = pltpu.get_barrier_semaphore()
    for dx, dy in XY:
        pl.semaphore_signal(barrier, inc=1, device_id=(sec, xydev(dx, dy)), device_id_type=MESH)
    pl.semaphore_signal(barrier, inc=1, device_id=sibling, device_id_type=MESH)
    for k in range(1, NZ):
        pl.semaphore_signal(barrier, inc=1, device_id=zdev(k, c), device_id_type=MESH)

    loads = []
    for h in range(2):
        first = pl.ds(pl.multiple_of(half * lax.rem(c + h, 2), half), half)
        loads.append(pltpu.make_async_copy(wg_hbm.at[0, first, :], wg.at[h], w_sem.at[2 * h]))
        loads.append(pltpu.make_async_copy(wu_hbm.at[0, first, :], wu.at[h], w_sem.at[2 * h + 1]))
    down_loads = []
    for k in range(NZ):
        cols = pl.ds(pl.multiple_of(chunk * rel(z + k), chunk), chunk)
        down_loads.append(pltpu.make_async_copy(wd_hbm.at[0, :, cols], wd.at[k], w_sem.at[4 + k]))
    for load in loads + down_loads:
        load.start()

    values = tok[...].astype(F32)
    average = jnp.mean(values, axis=-1, keepdims=True)
    centered = values - average
    variance = jnp.mean(centered * centered, axis=-1, keepdims=True)
    result = (centered * lax.rsqrt(variance + 1e-05) * gain[...]).astype(BF)
    normed[0] = result[:, :half]
    normed[1] = result[:, half:]

    toks = tok.shape[0]
    e_iota = lax.broadcasted_iota(jnp.int32, (experts, toks), 0)
    named = jnp.zeros((experts, toks), jnp.bool_)
    weight = jnp.zeros((experts, toks), F32)
    for k in range(ids.shape[0]):
        hit = e_iota == ids[k : k + 1, :]
        named = named | hit
        weight = weight + jnp.where(hit, gates[k : k + 1, :], 0.0)
    earlier = lax.broadcasted_iota(jnp.int32, (toks, toks), 0) < lax.broadcasted_iota(jnp.int32, (toks, toks), 1)
    named_f = jnp.where(named, 1.0, 0.0)
    slot = jnp.dot(named_f.astype(BF), jnp.where(earlier, 1.0, 0.0).astype(BF), preferred_element_type=F32)
    slot = jnp.where(named, slot, -1.0)
    s_iota = lax.broadcasted_iota(jnp.int32, (SLOTS, toks), 0).astype(F32)
    for j in range(BATCHES):
        for e in range(experts):
            here = (slot[e : e + 1, :] - float(SLOTS * j)) == s_iota
            lines = pl.ds(SLOTS * e, SLOTS)
            sel[j, lines, :] = jnp.where(here, 1.0, 0.0).astype(BF)
            share = jnp.where(here, weight[e : e + 1, :], 0.0)
            top = share.astype(BF)
            chi[j, lines, :] = top
            clo[j, lines, :] = (share - top.astype(F32)).astype(BF)

    mine = pl.ds(pl.multiple_of(SLOTS * me, SLOTS), SLOTS)

    def pack(j):
        packed[j] = jnp.dot(sel[j], normed[c], preferred_element_type=F32).astype(BF)
        xin[j, 0, mine, :] = packed[j, mine, :]

    def dispatch(j):
        copies = []
        for o, (dx, dy) in enumerate(XY):
            to = xydev(dx, dy)
            src = pl.ds(pl.multiple_of(SLOTS * to, SLOTS), SLOTS)
            copies.append(pltpu.make_async_remote_copy(
                src_ref=packed.at[j, src, :], dst_ref=xin.at[j, 0, mine, :],
                send_sem=xs.at[j, o], recv_sem=xr.at[j, o],
                device_id=(sec, to), device_id_type=MESH))
        return copies

    sent = []

    def start(copies):
        for copy in copies:
            copy.start()
            sent.append(copy)
        return copies

    pack(0)
    pl.semaphore_wait(barrier, len(XY) + NZ)
    arrivals = {0: start(dispatch(0))}
    pack(1)
    arrivals[1] = start(dispatch(1))
    pack(2)
    pack(3)

    def sib_x(j):
        return pltpu.make_async_remote_copy(
            src_ref=xin.at[j, 0], dst_ref=xin.at[j, 1], send_sem=fs.at[j], recv_sem=fr.at[j],
            device_id=sibling, device_id_type=MESH)

    own_rows = pl.ds(pl.multiple_of(hrows * c, hrows), hrows)
    sib_rows = pl.ds(pl.multiple_of(hrows * (1 - c), hrows), hrows)

    def sib_p(j, k):
        return pltpu.make_async_remote_copy(
            src_ref=part.at[j, k, sib_rows, :], dst_ref=sib.at[j, k], send_sem=ps.at[j, k], recv_sem=pr.at[j, k],
            device_id=sibling, device_id_type=MESH)

    def chain_a(j, t):
        return pltpu.make_async_remote_copy(
            src_ref=asend.at[j, t], dst_ref=arecv.at[j, t], send_sem=as_.at[j, t], recv_sem=ar.at[j, t],
            device_id=zdev(-sigma, c), device_id_type=MESH)

    def chain_b(j, t):
        return pltpu.make_async_remote_copy(
            src_ref=bsend.at[j, t], dst_ref=brecv.at[j, t], send_sem=bs.at[j, t], recv_sem=br.at[j, t],
            device_id=zdev(sigma, c), device_id_type=MESH)

    def own_sum(j, k):
        return part[j, k, own_rows, :].astype(F32) + sib[j, k].astype(F32)

    def rs_step(j, t):
        if j < 0 or j >= BATCHES:
            return
        ka, kb = rel(4 + sigma * t), rel(4 - sigma * (1 + t))
        if t == 0:
            for k in ORDER:
                sib_p(j, k).wait_recv()
        total = own_sum(j, ka)
        if t > 0:
            chain_a(j, t - 1).wait_recv()
            total = total + arecv[j, t - 1].astype(F32)
        asend[j, t] = total.astype(BF)
        start([chain_a(j, t)])
        if t < 3:
            total = own_sum(j, kb)
            if t > 0:
                chain_b(j, t - 1).wait_recv()
                total = total + brecv[j, t - 1].astype(F32)
            bsend[j, t] = total.astype(BF)
            start([chain_b(j, t)])

    def back(j, i):
        b = c * (experts // 2) + i
        return b, pltpu.make_async_remote_copy(
            src_ref=ret_out.at[j, pl.ds(SLOTS * i, SLOTS), :], dst_ref=ret.at[j, mine, :],
            send_sem=rs.at[j, i], recv_sem=rr.at[j, me], device_id=(sec, b), device_id_type=MESH)

    def rs_final(j):
        if j < 0 or j >= BATCHES:
            return
        chain_a(j, 3).wait_recv()
        chain_b(j, 2).wait_recv()
        total = own_sum(j, 0) + arecv[j, 3].astype(F32) + brecv[j, 2].astype(F32)
        ret_out[j] = total.astype(BF)
        for i in range(experts // 2):
            b, copy = back(j, i)

            @pl.when(b != me)
            def _():
                copy.start()

            @pl.when(b == me)
            def _():
                ret[j, mine, :] = ret_out[j, pl.ds(SLOTS * i, SLOTS), :]

    home = c == me // (experts // 2)

    def mix(j):
        if j < 0 or j >= BATCHES:
            return

        @pl.when(home)
        def _():
            for e in range(experts):
                @pl.when(e != me)
                def _():
                    lines = pl.ds(SLOTS * e, SLOTS)
                    pltpu.make_async_remote_copy(
                        src_ref=ret_out.at[j, pl.ds(0, SLOTS), :], dst_ref=ret.at[j, lines, :],
                        send_sem=rs.at[j, 0], recv_sem=rr.at[j, e],
                        device_id=sibling, device_id_type=MESH).wait_recv()
            dims = (((0,), (0,)), ((), ()))
            term = lax.dot_general(chi[j], ret[j], dims, preferred_element_type=F32)
            term = term + lax.dot_general(clo[j], ret[j], dims, preferred_element_type=F32)
            acc[...] = term if j == 0 else acc[...] + term

    def take(j):
        for copy in arrivals[j]:
            copy.wait_recv()
        if j + 2 < BATCHES:
            arrivals[j + 2] = start(dispatch(j + 2))
        start([sib_x(j)])

    def up(j, h):
        gate = jnp.dot(xin[j, h], wg[h], preferred_element_type=F32)
        raised = jnp.dot(xin[j, h], wu[h], preferred_element_type=F32)
        if h == 0:
            gacc[...] = gate
            uacc[...] = raised
            return None
        gate = gacc[...] + gate
        raised = uacc[...] + raised
        return (gate / (1.0 + jnp.exp(-gate)) * raised).astype(BF)

    def down(j, hidden):
        for k in ORDER:
            part[j, k] = jnp.dot(hidden, wd[k], preferred_element_type=F32).astype(BF)
            start([sib_p(j, k)])

    for j in range(BATCHES):
        rs_step(j - 1, 1)
        rs_step(j - 2, 3)
        take(j)
        if j == 0:
            loads[0].wait()
            loads[1].wait()
        up(j, 0)
        if j == 0:
            loads[2].wait()
            loads[3].wait()
        sib_x(j).wait_recv()
        hidden = up(j, 1)
        rs_step(j - 1, 2)
        rs_final(j - 2)
        if j == 0:
            for load in down_loads:
                load.wait()
        down(j, hidden)
        rs_step(j, 0)
        mix(j - 3)
    last = BATCHES - 1
    rs_step(last, 1)
    rs_step(last - 1, 3)
    rs_step(last, 2)
    rs_final(last - 1)
    mix(last - 2)
    rs_step(last, 3)
    mix(last - 1)
    rs_final(last)
    mix(last)

    def give(k):
        return pltpu.make_async_remote_copy(
            src_ref=mixed.at[z], dst_ref=mixed.at[z], send_sem=os_.at[k], recv_sem=or_.at[k],
            device_id=zdev(k, c), device_id_type=MESH)

    def hand(k):
        at = rel(z + k)
        return pltpu.make_async_remote_copy(
            src_ref=mixed.at[at], dst_ref=mixed.at[at], send_sem=gs.at[k], recv_sem=gr.at[k],
            device_id=sibling, device_id_type=MESH)

    @pl.when(home)
    def _():
        mixed[z] = acc[...].astype(BF)
        for k in (1, 7, 2, 6, 3, 5, 4):
            give(k).start()
        hand(0).start()
        for k in (1, 7, 2, 6, 3, 5, 4):
            give(k).wait_recv()
            hand(NZ - k).start()
        for k in range(1, NZ):
            give(k).wait_send()
        for k in range(NZ):
            hand(k).wait_send()

    @pl.when(jnp.logical_not(home))
    def _():
        for k in range(NZ):
            hand(k).wait_recv()

    for k in range(NZ):
        out[:, chunk * k : chunk * (k + 1)] = mixed[k]
    for copy in sent:
        copy.wait_send()
    for j in range(BATCHES):
        for i in range(experts // 2):
            b, copy = back(j, i)

            @pl.when(b != me)
            def _():
                copy.wait_send()


def on_device(tokens, norm_gain, expert_ids, gates, gate_proj, up_proj, down_proj):
    toks, features = tokens.shape
    experts = lax.axis_size("expert")
    width = gate_proj.shape[2]
    half, chunk = features // 2, features // NZ
    rows = experts * SLOTS
    dma = pltpu.SemaphoreType.DMA
    vmem = pl.BlockSpec(memory_space=pltpu.VMEM)
    hbm = pl.BlockSpec(memory_space=pl.ANY)
    b = BATCHES
    scratch = [
        pltpu.VMEM((2, half, width), BF),
        pltpu.VMEM((2, half, width), BF),
        pltpu.VMEM((NZ, width, chunk), BF),
        pltpu.VMEM((2, toks, half), BF),
        pltpu.VMEM((b, rows, toks), BF),
        pltpu.VMEM((b, rows, toks), BF),
        pltpu.VMEM((b, rows, toks), BF),
        pltpu.VMEM((b, rows, half), BF),
        pltpu.VMEM((b, 2, rows, half), BF),
        pltpu.VMEM((rows, width), F32),
        pltpu.VMEM((rows, width), F32),
        pltpu.VMEM((b, NZ, rows, chunk), BF),
        pltpu.VMEM((b, NZ, rows // 2, chunk), BF),
        pltpu.VMEM((b, 4, rows // 2, chunk), BF),
        pltpu.VMEM((b, 4, rows // 2, chunk), BF),
        pltpu.VMEM((b, 3, rows // 2, chunk), BF),
        pltpu.VMEM((b, 3, rows // 2, chunk), BF),
        pltpu.VMEM((b, rows // 2, chunk), BF),
        pltpu.VMEM((b, rows, chunk), BF),
        pltpu.VMEM((toks, chunk), F32),
        pltpu.VMEM((NZ, toks, chunk), BF),
        dma((4 + NZ,)),
        dma((b, len(XY))), dma((b, len(XY))),
        dma((b,)), dma((b,)),
        dma((b, NZ)), dma((b, NZ)),
        dma((b, 4)), dma((b, 4)),
        dma((b, 3)), dma((b, 3)),
        dma((b, experts // 2)), dma((b, experts)),
        dma((NZ,)), dma((NZ,)),
        dma((NZ,)), dma((NZ,)),
    ]
    return pl.pallas_call(
        kernel,
        out_shape=jax.ShapeDtypeStruct((toks, features), BF),
        in_specs=[vmem, vmem, vmem, vmem, hbm, hbm, hbm],
        out_specs=vmem,
        scratch_shapes=scratch,
        compiler_params=pltpu.CompilerParams(
            collective_id=0, has_side_effects=True, vmem_limit_bytes=60 << 20
        ),
    )(tokens, norm_gain.reshape(1, -1), expert_ids.T, gates.T, gate_proj, up_proj, down_proj)


def solution(mesh):
    return jax.shard_map(
        on_device,
        mesh=mesh,
        in_specs=(
            P("expert", None),
            P(),
            P("expert", None),
            P("expert", None),
            P("expert", None, "section"),
            P("expert", None, "section"),
            P("expert", "section", None),
        ),
        out_specs=P("expert", None),
        check_vma=False,
    )
```

```python
import jax
import jax.numpy as jnp
from jax import lax
from jax.experimental import pallas as pl
from jax.experimental.pallas import tpu as pltpu
from jax.sharding import PartitionSpec as P

MESH = pl.DeviceIdType.MESH
BATCHES = 4
ALONE = 2
SLOTS = 16
NZ = 8
SIDE = 4
XY = [(dx, dy) for dx in range(SIDE) for dy in range(SIDE) if (dx, dy) != (0, 0)]
ORDER = ((4, 3, 5, 2), (6, 1, 7, 0))
PLACE = {k: (g, i) for g, ks in enumerate(ORDER) for i, k in enumerate(ks)}
PIECES = 3
BF = jnp.bfloat16
F32 = jnp.float32


def kernel(
    tok, gain, ids, gates, wg_hbm, wu_hbm, wd_hbm, out,
    wg, wu, wd, line, slots, chi, clo, chi2, clo2, packed, xin, gacc, uacc, part, sib,
    asend, arecv, bsend, brecv, asend2, arecv2, bsend2, brecv2, ret_out, ret, ret_out2, ret2, acc, mixed,
    w_sem, ls, lr, ns, nr, xs, xr, fs, fr, ps, pr, as_, ar, bs, br, as2, ar2, bs2, br2, rs, rr, rr2, os_, or_, gs, gr,
):
    sec, me = lax.axis_index("section"), lax.axis_index("expert")
    z, c = sec // 2, sec % 2
    x, y = me // SIDE, me % SIDE
    experts = SIDE * SIDE
    blocks = experts // 2
    toks = tok.shape[0]
    htoks = toks // 2
    fine = line.shape[3]
    half = fine * PIECES
    col = mixed.shape[3]
    chunk = col * PIECES
    hrows = blocks * SLOTS
    late = BATCHES - ALONE
    first_step, then_step = SIDE * (1 - c) + c, SIDE * c + (1 - c)
    first_at, then_at = x * (1 - c) + y * c, y * (1 - c) + x * c

    def on_first(i):
        return me + (i - first_at) * first_step

    def on_then(i):
        return me + (i - then_at) * then_step

    def zdev(dz):
        return (lax.rem(z + dz + 2 * NZ, NZ) * 2 + c, me)

    def xydev(dx, dy):
        return lax.rem(x + dx, SIDE) * SIDE + lax.rem(y + dy, SIDE)

    other = z * 2 + 1 - c
    sibling = (other, me)

    barrier = pltpu.get_barrier_semaphore()
    for dx, dy in XY:
        for s in (sec, other):
            pl.semaphore_signal(barrier, inc=1, device_id=(s, xydev(dx, dy)), device_id_type=MESH)
    pl.semaphore_signal(barrier, inc=1, device_id=sibling, device_id_type=MESH)
    for k in range(1, NZ):
        pl.semaphore_signal(barrier, inc=1, device_id=zdev(k), device_id_type=MESH)

    loads = []
    for h in range(2):
        lines = pl.ds(pl.multiple_of(half * lax.rem(c + h, 2), half), half)
        loads.append(pltpu.make_async_copy(wg_hbm.at[0, lines, :], wg.at[h], w_sem.at[2 * h]))
        loads.append(pltpu.make_async_copy(wu_hbm.at[0, lines, :], wu.at[h], w_sem.at[2 * h + 1]))
    for load in loads:
        load.start()
    for k in range(NZ):
        cols = pl.ds(pl.multiple_of(chunk * lax.rem(z + k, NZ), chunk), chunk)
        g, i = PLACE[k]
        pltpu.make_async_copy(wd_hbm.at[0, :, cols], wd.at[g, :, pl.ds(chunk * i, chunk)], w_sem.at[4]).start()

    def await_bytes(ref, sem):
        pltpu.make_async_copy(ref, ref, sem).wait()

    e_iota = lax.broadcasted_iota(jnp.int32, (experts, toks), 0)
    named = jnp.zeros((experts, toks), jnp.bool_)
    weight = jnp.zeros((experts, toks), F32)
    for k in range(ids.shape[0]):
        hit = e_iota == ids[k : k + 1, :]
        named = named | hit
        weight = weight + jnp.where(hit, gates[k : k + 1, :], 0.0)
    earlier = lax.broadcasted_iota(jnp.int32, (toks, toks), 0) < lax.broadcasted_iota(jnp.int32, (toks, toks), 1)
    slot = jnp.dot(
        jnp.where(named, 1.0, 0.0).astype(BF), jnp.where(earlier, 1.0, 0.0).astype(BF), preferred_element_type=F32)
    slot = jnp.where(named, slot, -1.0)
    slots[first_at] = slot

    with jax.named_scope("norm"):
        values = tok[...].astype(F32)
        average = jnp.mean(values, axis=-1, keepdims=True)
        centered = values - average
        variance = jnp.mean(centered * centered, axis=-1, keepdims=True)
        normed = (centered * lax.rsqrt(variance + 1e-05) * gain[...]).astype(BF)
        for cc in range(2):
            @pl.when(c == cc)
            def _():
                for f in range(PIECES):
                    line[f, first_at] = normed[:, half * cc + fine * f : half * cc + fine * (f + 1)]

    def remote(src, dst, send_sem, recv_sem, to):
        return pltpu.make_async_remote_copy(
            src_ref=src, dst_ref=dst, send_sem=send_sem, recv_sem=recv_sem, device_id=to, device_id_type=MESH)

    with jax.named_scope("entry_wait"):
        pl.semaphore_wait(barrier, 2 * len(XY) + NZ)
    mates = [(sec, on_first(lax.rem(first_at + k, SIDE))) for k in (1, 3, 2)]
    for to in mates:
        remote(slots.at[first_at], slots.at[first_at], ns.at[0], nr.at[0], to).start()
    for f in range(PIECES):
        for to in mates:
            remote(line.at[f, first_at], line.at[f, first_at], ls.at[0], lr.at[f], to).start()

    def shares(low, count, hi, lo):
        places = lax.broadcasted_iota(jnp.int32, (count, toks), 0).astype(F32) + float(low)
        rows = [jnp.where(slot[e : e + 1, :] == places, weight[e : e + 1, :], 0.0) for e in range(experts)]
        share = jnp.transpose(jnp.concatenate(rows, axis=0))
        top = share.astype(BF)
        hi[...] = top
        lo[...] = (share - top.astype(F32)).astype(BF)

    with jax.named_scope("shares"):
        for j in range(ALONE):
            shares(SLOTS * j, SLOTS, chi.at[j], clo.at[j])
        shares(SLOTS * ALONE, SLOTS * late, chi2, clo2)

    def block_rows(i):
        return pl.ds(pl.multiple_of(SLOTS * on_first(i), SLOTS), SLOTS)

    s_iota = lax.broadcasted_iota(jnp.int32, (SLOTS, toks), 0).astype(F32)

    def picks(js, i):
        rows = []
        for j in js:
            for q in range(SIDE):
                row = slots[i, pl.ds(on_then(q), 1), :]
                rows.append(jnp.where((row - float(SLOTS * j)) == s_iota, 1.0, 0.0).astype(BF))
        return jnp.concatenate(rows, axis=0)

    @jax.named_scope("pack")
    def pack(js, f):
        cols = slice(fine * f, fine * (f + 1))
        for i in range(SIDE):
            rows = jnp.dot(picks(js, i), line[f, i], preferred_element_type=F32).astype(BF)
            for n, j in enumerate(js):
                for q in range(SIDE):
                    at = SLOTS * (n * SIDE + q)
                    packed[j, q, i, :, cols] = rows[at : at + SLOTS, :]
        for j in js:
            for i in range(SIDE):
                xin[j, 0, block_rows(i), cols] = packed[j, then_at, i, :, cols]

    def dispatch(j, cols):
        for k in (1, 3, 2):
            q = lax.rem(then_at + k, SIDE)
            for i in range(SIDE):
                remote(
                    packed.at[j, q, i, :, cols], xin.at[j, 0, block_rows(i), cols], xs.at[0], xr.at[j],
                    (sec, on_then(q))).start()

    await_bytes(slots.at[pl.ds(0, SIDE - 1)], nr.at[0])
    for f in range(PIECES):
        with jax.named_scope("line_wait"):
            await_bytes(line.at[f, pl.ds(0, SIDE - 1)], lr.at[f])
        pack([0], f)
        dispatch(0, pl.ds(fine * f, fine))
    for f in range(PIECES):
        pack(list(range(1, BATCHES)), f)
    every = pl.ds(0, half)
    dispatch(1, every)

    def sib_x(j):
        return remote(xin.at[j, 0], xin.at[j, 1], fs.at[0], fr.at[j], sibling)

    own_rows = pl.ds(pl.multiple_of(hrows * c, hrows), hrows)
    sib_rows = pl.ds(pl.multiple_of(hrows * (1 - c), hrows), hrows)

    def sib_p(j, g):
        return remote(part.at[j, g, sib_rows, :], sib.at[j, g], ps.at[0], pr.at[j, g], sibling)

    def own_sum(j, k, first, count):
        g, i = PLACE[k % NZ]
        cols = slice(chunk * i + first, chunk * i + first + count)
        return part[j, g, own_rows, cols].astype(F32) + sib[j, g, :, cols].astype(F32)

    def sign(j):
        return 1 - 2 * (j % 2)

    def chain_a(j, t):
        return remote(asend.at[j, t], arecv.at[j, t], as_.at[0], ar.at[j, t], zdev(-sign(j)))

    def chain_b(j, t):
        return remote(bsend.at[j, t], brecv.at[j, t], bs.at[0], br.at[j, t], zdev(sign(j)))

    @jax.named_scope("chain_step")
    def chain_step(j, t):
        if j < 0 or j >= ALONE:
            return
        ka, kb = 4 + sign(j) * t, 4 - sign(j) * (1 + t)
        if t < 2:
            sib_p(j, t).wait_recv()
        total = own_sum(j, ka, 0, chunk)
        if t > 0:
            chain_a(j, t - 1).wait_recv()
            total = total + arecv[j, t - 1].astype(F32)
        asend[j, t] = total.astype(BF)
        chain_a(j, t).start()
        if t < 3:
            total = own_sum(j, kb, 0, chunk)
            if t > 0:
                chain_b(j, t - 1).wait_recv()
                total = total + brecv[j, t - 1].astype(F32)
            bsend[j, t] = total.astype(BF)
            chain_b(j, t).start()

    def late_a(p, t):
        return remote(asend2.at[p, t], arecv2.at[p, t], as2.at[0], ar2.at[p, t], zdev(-sign(p)))

    def late_b(p, t):
        return remote(bsend2.at[p, t], brecv2.at[p, t], bs2.at[0], br2.at[p, t], zdev(sign(p)))

    @jax.named_scope("late_step")
    def late_step(p, t):
        ka, kb = 4 + sign(p) * t, 4 - sign(p) * (1 + t)
        if p == 0 and t < 2:
            for j in range(ALONE, BATCHES):
                sib_p(j, t).wait_recv()
        for k, send, recv, step in ((ka, asend2, arecv2, late_a), (kb, bsend2, brecv2, late_b)):
            if send is bsend2 and t == 3:
                continue
            if t > 0:
                step(p, t - 1).wait_recv()
            for n in range(late):
                lines = slice(hrows * n, hrows * (n + 1))
                total = own_sum(ALONE + n, k, col * p, col)
                if t > 0:
                    total = total + recv[p, t - 1, lines, :].astype(F32)
                send[p, t, lines, :] = total.astype(BF)
            step(p, t).start()

    def give_back(src, dst, height, send_sem, recv_sem):
        mine = pl.ds(pl.multiple_of(height * me, height), height)
        for i in range(blocks):
            b = c * blocks + i
            rows = pl.ds(height * i, height)

            @pl.when(b != me)
            def _():
                remote(src.at[rows, :], dst.at[mine, :], send_sem, recv_sem, (sec, b)).start()

            @pl.when(b == me)
            def _():
                dst[mine, :] = src[rows, :]

            remote(src.at[rows, :], dst.at[mine, :], send_sem, recv_sem, (other, b)).start()

    home = c == me // blocks

    def await_rows(ref, height, sem):
        @pl.when(home)
        def _():
            await_bytes(ref.at[pl.ds(0, height * (experts - 1)), :], sem)

        @pl.when(jnp.logical_not(home))
        def _():
            await_bytes(ref, sem)

    @jax.named_scope("chain_end")
    def chain_end(j):
        chain_a(j, 3).wait_recv()
        chain_b(j, 2).wait_recv()
        total = own_sum(j, 0, 0, chunk) + arecv[j, 3].astype(F32) + brecv[j, 2].astype(F32)
        ret_out[j] = total.astype(BF)
        give_back(ret_out.at[j], ret.at[j], SLOTS, rs.at[j], rr.at[j])

    @jax.named_scope("late_end")
    def late_end(p):
        late_a(p, 3).wait_recv()
        late_b(p, 2).wait_recv()
        for n in range(late):
            lines = slice(hrows * n, hrows * (n + 1))
            total = own_sum(ALONE + n, 0, col * p, col)
            total = total + arecv2[p, 3, lines, :].astype(F32) + brecv2[p, 2, lines, :].astype(F32)
            total = total.astype(BF)
            for i in range(blocks):
                at = SLOTS * (late * i + n)
                ret_out2[p, at : at + SLOTS, :] = total[SLOTS * i : SLOTS * (i + 1), :]
        give_back(ret_out2.at[p], ret2.at[p], SLOTS * late, rs.at[ALONE + p], rr2.at[p])

    own_toks = pl.ds(pl.multiple_of(htoks * c, htoks), htoks)

    @jax.named_scope("mix")
    def mix(j):
        await_rows(ret.at[j], SLOTS, rr.at[j])
        term = jnp.dot(chi[j], ret[j], preferred_element_type=F32)
        term = term + jnp.dot(clo[j], ret[j], preferred_element_type=F32)
        acc[...] = term if j == 0 else acc[...] + term

    def give(p, k):
        here = mixed.at[p, z, own_toks, :]
        return remote(here, here, os_.at[0], or_.at[p], zdev(k))

    def hand(p):
        here = mixed.at[p, :, own_toks, :]
        return remote(here, here, gs.at[0], gr.at[p], sibling)

    @jax.named_scope("late_mix")
    def late_mix(p):
        await_rows(ret2.at[p], SLOTS * late, rr2.at[p])
        term = jnp.dot(chi2[...], ret2[p], preferred_element_type=F32)
        term = term + jnp.dot(clo2[...], ret2[p], preferred_element_type=F32)
        cols = slice(col * p, col * (p + 1))
        acc[:, cols] = acc[:, cols] + term
        mixed[p, z, own_toks, :] = acc[own_toks, cols].astype(BF)
        for k in (4, 3, 5, 2, 6, 1, 7):
            give(p, k).start()

    @jax.named_scope("take")
    def take(j):
        if j >= BATCHES:
            return
        await_bytes(xin.at[j, 0, pl.ds(0, SLOTS * SIDE * (SIDE - 1)), :], xr.at[j])
        if j + 2 < BATCHES:
            dispatch(j + 2, every)
        sib_x(j).start()

    @jax.named_scope("up")
    def up(j, h):
        gate = jnp.dot(xin[j, h], wg[h], preferred_element_type=F32)
        raised = jnp.dot(xin[j, h], wu[h], preferred_element_type=F32)
        if h == 0:
            gacc[...] = gate
            uacc[...] = raised
            return None
        gate = gacc[...] + gate
        raised = uacc[...] + raised
        return (gate / (1.0 + jnp.exp(-gate)) * raised).astype(BF)

    @jax.named_scope("down")
    def down(j, hidden):
        for g in range(2):
            part[j, g] = jnp.dot(hidden, wd[g], preferred_element_type=F32).astype(BF)
            sib_p(j, g).start()

    take(0)
    for j in range(BATCHES):
        if j == 0:
            loads[0].wait()
            loads[1].wait()
        up(j, 0)
        if j == 0:
            loads[2].wait()
            loads[3].wait()
        with jax.named_scope("sib_wait"):
            sib_x(j).wait_recv()
        hidden = up(j, 1)
        if j == 0:
            await_bytes(wd, w_sem.at[4])
        down(j, hidden)
        take(j + 1)
        for t in range(1, 4):
            chain_step(j - t, t)
        chain_step(j, 0)
    for p in range(PIECES):
        late_step(p, 0)
    for p in range(PIECES):
        late_step(p, 1)
    chain_step(1, 3)
    chain_end(0)
    for p in range(PIECES):
        late_step(p, 2)
    chain_end(1)
    mix(0)
    for p in range(PIECES):
        late_step(p, 3)
    mix(1)
    for p in range(PIECES):
        late_end(p)
    for p in range(PIECES):
        late_mix(p)

    with jax.named_scope("drain"):
        await_bytes(slots.at[pl.ds(0, SIDE - 1)], ns.at[0])
        await_bytes(line.at[:, pl.ds(0, SIDE - 1)], ls.at[0])
        await_bytes(packed.at[:, pl.ds(0, SIDE - 1)], xs.at[0])
        await_bytes(xin.at[:, 0], fs.at[0])
        await_bytes(part.at[:, :, pl.ds(0, hrows), :], ps.at[0])
        await_bytes(asend, as_.at[0])
        await_bytes(bsend, bs.at[0])
        await_bytes(asend2, as2.at[0])
        await_bytes(bsend2, bs2.at[0])
        for j in range(ALONE):
            await_rows(ret.at[j], SLOTS, rs.at[j])
        for p in range(PIECES):
            await_rows(ret2.at[p], SLOTS * late, rs.at[ALONE + p])
    for p in range(PIECES):
        with jax.named_scope("gather_wait"):
            await_bytes(mixed.at[p, pl.ds(0, NZ - 1), pl.ds(0, htoks), :], or_.at[p])
        hand(p).start()
    for p in range(PIECES):
        with jax.named_scope("hand_wait"):
            hand(p).wait_recv()
        for k in range(NZ):
            out[:, chunk * k + col * p : chunk * k + col * (p + 1)] = mixed[p, k]
    await_bytes(mixed.at[:, pl.ds(0, NZ - 1), pl.ds(0, htoks), :], os_.at[0])
    await_bytes(mixed.at[:, :, pl.ds(0, htoks), :], gs.at[0])


def on_device(tokens, norm_gain, expert_ids, gates, gate_proj, up_proj, down_proj):
    toks, features = tokens.shape
    experts = lax.axis_size("expert")
    width = gate_proj.shape[2]
    half, chunk = features // 2, features // NZ
    fine, col = half // PIECES, chunk // PIECES
    rows = experts * SLOTS
    hrows = rows // 2
    late = BATCHES - ALONE
    dma = pltpu.SemaphoreType.DMA
    vmem = pl.BlockSpec(memory_space=pltpu.VMEM)
    hbm = pl.BlockSpec(memory_space=pl.ANY)
    b = BATCHES
    scratch = [
        pltpu.VMEM((2, half, width), BF),
        pltpu.VMEM((2, half, width), BF),
        pltpu.VMEM((2, width, half), BF),
        pltpu.VMEM((PIECES, SIDE, toks, fine), BF),
        pltpu.VMEM((SIDE, experts, toks), F32),
        pltpu.VMEM((ALONE, toks, rows), BF),
        pltpu.VMEM((ALONE, toks, rows), BF),
        pltpu.VMEM((toks, rows * late), BF),
        pltpu.VMEM((toks, rows * late), BF),
        pltpu.VMEM((b, SIDE, SIDE, SLOTS, half), BF),
        pltpu.VMEM((b, 2, rows, half), BF),
        pltpu.VMEM((rows, width), F32),
        pltpu.VMEM((rows, width), F32),
        pltpu.VMEM((b, 2, rows, half), BF),
        pltpu.VMEM((b, 2, hrows, half), BF),
        pltpu.VMEM((ALONE, 4, hrows, chunk), BF),
        pltpu.VMEM((ALONE, 4, hrows, chunk), BF),
        pltpu.VMEM((ALONE, 3, hrows, chunk), BF),
        pltpu.VMEM((ALONE, 3, hrows, chunk), BF),
        pltpu.VMEM((PIECES, 4, hrows * late, col), BF),
        pltpu.VMEM((PIECES, 4, hrows * late, col), BF),
        pltpu.VMEM((PIECES, 3, hrows * late, col), BF),
        pltpu.VMEM((PIECES, 3, hrows * late, col), BF),
        pltpu.VMEM((ALONE, hrows, chunk), BF),
        pltpu.VMEM((ALONE, rows, chunk), BF),
        pltpu.VMEM((PIECES, hrows * late, col), BF),
        pltpu.VMEM((PIECES, rows * late, col), BF),
        pltpu.VMEM((toks, chunk), F32),
        pltpu.VMEM((PIECES, NZ, toks, col), BF),
        dma((5,)),
        dma((1,)), dma((PIECES,)),
        dma((1,)), dma((1,)),
        dma((1,)), dma((b,)),
        dma((1,)), dma((b,)),
        dma((1,)), dma((b, 2)),
        dma((1,)), dma((ALONE, 4)),
        dma((1,)), dma((ALONE, 3)),
        dma((1,)), dma((PIECES, 4)),
        dma((1,)), dma((PIECES, 3)),
        dma((ALONE + PIECES,)), dma((ALONE,)), dma((PIECES,)),
        dma((1,)), dma((PIECES,)),
        dma((1,)), dma((PIECES,)),
    ]
    return pl.pallas_call(
        kernel,
        out_shape=pltpu.VMEM((toks, features), BF),
        in_specs=[vmem, vmem, vmem, vmem, hbm, hbm, hbm],
        out_specs=vmem,
        scratch_shapes=scratch,
        compiler_params=pltpu.CompilerParams(
            collective_id=0, has_side_effects=True, vmem_limit_bytes=60 << 20
        ),
    )(tokens, norm_gain.reshape(1, -1), expert_ids.T, gates.T, gate_proj, up_proj, down_proj)


def solution(mesh):
    return jax.shard_map(
        on_device,
        mesh=mesh,
        in_specs=(
            P("expert", None),
            P(),
            P("expert", None),
            P("expert", None),
            P("expert", None, "section"),
            P("expert", None, "section"),
            P("expert", "section", None),
        ),
        out_specs=P("expert", None),
        check_vma=False,
    )
```

```python
import jax
import jax.numpy as jnp
from jax import lax
from jax.experimental import pallas as pl
from jax.experimental.pallas import tpu as pltpu
from jax.sharding import PartitionSpec as P

MESH = pl.DeviceIdType.MESH
BATCHES = 4
CHAINS = 2
SLOTS = 16
NZ = 8
SIDE = 4
XY = [(dx, dy) for dx in range(SIDE) for dy in range(SIDE) if (dx, dy) != (0, 0)]
ORDER = ((4, 3, 5, 2), (6, 1, 7, 0))
PLACE = {k: (g, i) for g, ks in enumerate(ORDER) for i, k in enumerate(ks)}
PIECES = 3
PARTS = 2
BF = jnp.bfloat16
F32 = jnp.float32


def kernel(
    tok, gain, ids, gates, wg_hbm, wu_hbm, wd_hbm, out,
    wg, wu, wd, line, slots, chi, clo, packed, xin, gacc, uacc, part, sib,
    asend, arecv, bsend, brecv, ret_out, ret, late_out, late_in, zsend, zrecv, acc, mixed,
    w_sem, ls, lr, ns, nr, xs, xr, fs, fr, ps, pr, as_, ar, bs, br, rs, rr, rl, zs, zr, os_, or_, gs, gr,
):
    sec, me = lax.axis_index("section"), lax.axis_index("expert")
    z, c = sec // 2, sec % 2
    x, y = me // SIDE, me % SIDE
    experts = SIDE * SIDE
    blocks = experts // 2
    toks = tok.shape[0]
    htoks = toks // 2
    fine = line.shape[4]
    wide = fine * PARTS
    half = 2 * wide
    col = mixed.shape[3]
    chunk = col * PIECES
    hrows = blocks * SLOTS
    first_at, then_at = (x, y), (y, x)

    def on_first(f, i):
        return i * SIDE + y if f == 0 else x * SIDE + i

    def on_then(f, q):
        return x * SIDE + q if f == 0 else q * SIDE + y

    def zdev(dz, core=c):
        return (lax.rem(z + dz + 2 * NZ, NZ) * 2 + core, me)

    def xydev(dx, dy):
        return lax.rem(x + dx, SIDE) * SIDE + lax.rem(y + dy, SIDE)

    other = z * 2 + 1 - c
    sibling = (other, me)

    barrier = pltpu.get_barrier_semaphore()
    for dx, dy in XY:
        for s in (sec, other):
            pl.semaphore_signal(barrier, inc=1, device_id=(s, xydev(dx, dy)), device_id_type=MESH)
    pl.semaphore_signal(barrier, inc=1, device_id=sibling, device_id_type=MESH)
    for k in range(1, NZ):
        for core in range(2):
            pl.semaphore_signal(barrier, inc=1, device_id=zdev(k, core), device_id_type=MESH)

    loads = []
    for h in range(2):
        lines = pl.ds(pl.multiple_of(half * lax.rem(c + h, 2), half), half)
        loads.append(pltpu.make_async_copy(wg_hbm.at[0, lines, :], wg.at[h], w_sem.at[2 * h]))
        loads.append(pltpu.make_async_copy(wu_hbm.at[0, lines, :], wu.at[h], w_sem.at[2 * h + 1]))
    for load in loads:
        load.start()
    for k in range(NZ):
        cols = pl.ds(pl.multiple_of(chunk * lax.rem(z + k, NZ), chunk), chunk)
        g, i = PLACE[k]
        pltpu.make_async_copy(wd_hbm.at[0, :, cols], wd.at[g, :, pl.ds(chunk * i, chunk)], w_sem.at[4]).start()

    def await_bytes(ref, sem):
        pltpu.make_async_copy(ref, ref, sem).wait()

    e_iota = lax.broadcasted_iota(jnp.int32, (experts, toks), 0)
    named = jnp.zeros((experts, toks), jnp.bool_)
    weight = jnp.zeros((experts, toks), F32)
    for k in range(ids.shape[0]):
        hit = e_iota == ids[k : k + 1, :]
        named = named | hit
        weight = weight + jnp.where(hit, gates[k : k + 1, :], 0.0)
    earlier = lax.broadcasted_iota(jnp.int32, (toks, toks), 0) < lax.broadcasted_iota(jnp.int32, (toks, toks), 1)
    slot = jnp.dot(
        jnp.where(named, 1.0, 0.0).astype(BF), jnp.where(earlier, 1.0, 0.0).astype(BF), preferred_element_type=F32)
    slot = jnp.where(named, slot, -1.0)
    for f in range(2):
        slots[f, first_at[f]] = slot

    with jax.named_scope("norm"):
        values = tok[...].astype(F32)
        average = jnp.mean(values, axis=-1, keepdims=True)
        centered = values - average
        variance = jnp.mean(centered * centered, axis=-1, keepdims=True)
        normed = (centered * lax.rsqrt(variance + 1e-05) * gain[...]).astype(BF)
        for cc in range(2):
            @pl.when(c == cc)
            def _():
                for f in range(2):
                    for s in range(PARTS):
                        at = half * cc + wide * f + fine * s
                        line[f, s, first_at[f]] = normed[:, at : at + fine]

    def remote(src, dst, send_sem, recv_sem, to):
        return pltpu.make_async_remote_copy(
            src_ref=src, dst_ref=dst, send_sem=send_sem, recv_sem=recv_sem, device_id=to, device_id_type=MESH)

    with jax.named_scope("entry_wait"):
        pl.semaphore_wait(barrier, 2 * len(XY) + 2 * NZ - 1)
    def mates(f):
        return [(sec, on_first(f, lax.rem(first_at[f] + k, SIDE))) for k in (1, 3, 2)]

    for f in range(2):
        for to in mates(f):
            here = slots.at[f, first_at[f]]
            remote(here, here, ns.at[0], nr.at[f], to).start()
    for s in range(PARTS):
        for f in range(2):
            for to in mates(f):
                here = line.at[f, s, first_at[f]]
                remote(here, here, ls.at[0], lr.at[f, s], to).start()

    def shares(low, count, hi, lo):
        places = lax.broadcasted_iota(jnp.int32, (count, toks), 0).astype(F32) + float(low)
        rows = [jnp.where(slot[e : e + 1, :] == places, weight[e : e + 1, :], 0.0) for e in range(experts)]
        share = jnp.transpose(jnp.concatenate(rows, axis=0))
        top = share.astype(BF)
        hi[...] = top
        lo[...] = (share - top.astype(F32)).astype(BF)

    with jax.named_scope("shares"):
        for j in range(BATCHES):
            shares(SLOTS * j, SLOTS, chi.at[j], clo.at[j])

    def block_rows(f, i):
        return pl.ds(pl.multiple_of(SLOTS * on_first(f, i), SLOTS), SLOTS)

    s_iota = lax.broadcasted_iota(jnp.int32, (SLOTS, toks), 0).astype(F32)

    def picks(js, f, i):
        rows = []
        for j in js:
            for q in range(SIDE):
                row = slots[f, i, pl.ds(on_then(f, q), 1), :]
                rows.append(jnp.where((row - float(SLOTS * j)) == s_iota, 1.0, 0.0).astype(BF))
        return jnp.concatenate(rows, axis=0)

    @jax.named_scope("pack")
    def pack(js, f, parts):
        for i in range(SIDE):
            chosen = picks(js, f, i)
            for s in parts:
                cols = slice(fine * s, fine * (s + 1))
                rows = jnp.dot(chosen, line[f, s, i], preferred_element_type=F32).astype(BF)
                for n, j in enumerate(js):
                    for q in range(SIDE):
                        at = SLOTS * (n * SIDE + q)
                        packed[j, f, q, i, :, cols] = rows[at : at + SLOTS, :]
        for j in js:
            for i in range(SIDE):
                for s in parts:
                    cols = slice(fine * s, fine * (s + 1))
                    to = slice(wide * f + fine * s, wide * f + fine * (s + 1))
                    xin[j, 0, block_rows(f, i), to] = packed[j, f, then_at[f], i, :, cols]

    def dispatch(j, f, first, count):
        for k in (1, 3, 2):
            q = lax.rem(then_at[f] + k, SIDE)
            for i in range(SIDE):
                remote(
                    packed.at[j, f, q, i, :, pl.ds(first, count)],
                    xin.at[j, 0, block_rows(f, i), pl.ds(wide * f + first, count)], xs.at[0], xr.at[j],
                    (sec, on_then(f, q))).start()

    for f in range(2):
        await_bytes(slots.at[f, pl.ds(0, SIDE - 1)], nr.at[f])
    for s in range(PARTS):
        for f in range(2):
            with jax.named_scope("line_wait"):
                await_bytes(line.at[f, s, pl.ds(0, SIDE - 1)], lr.at[f, s])
            pack([0], f, [s])
            dispatch(0, f, fine * s, fine)

    def dispatch_all(j):
        for f in range(2):
            dispatch(j, f, 0, wide)

    for f in range(2):
        pack(list(range(1, BATCHES)), f, range(PARTS))
    dispatch_all(1)

    def sib_x(j):
        return remote(xin.at[j, 0], xin.at[j, 1], fs.at[0], fr.at[j], sibling)

    own_rows = pl.ds(pl.multiple_of(hrows * c, hrows), hrows)
    sib_rows = pl.ds(pl.multiple_of(hrows * (1 - c), hrows), hrows)

    def sib_p(j, g):
        return remote(part.at[j, g, sib_rows, :], sib.at[j, g], ps.at[0], pr.at[j, g], sibling)

    def own_sum(j, k, first, count):
        g, i = PLACE[k % NZ]
        cols = slice(chunk * i + first, chunk * i + first + count)
        return part[j, g, own_rows, cols].astype(F32) + sib[j, g, :, cols].astype(F32)

    def sign(j):
        return 1 - 2 * (j % 2)

    def chain_a(j, t):
        return remote(asend.at[j, t], arecv.at[j, t], as_.at[0], ar.at[j, t], zdev(-sign(j)))

    def chain_b(j, t):
        return remote(bsend.at[j, t], brecv.at[j, t], bs.at[0], br.at[j, t], zdev(sign(j)))

    @jax.named_scope("chain_step")
    def chain_step(j, t):
        if j < 0 or j >= CHAINS:
            return
        ka, kb = 4 + sign(j) * t, 4 - sign(j) * (1 + t)
        if t < 2:
            sib_p(j, t).wait_recv()
        total = own_sum(j, ka, 0, chunk)
        if t > 0:
            chain_a(j, t - 1).wait_recv()
            total = total + arecv[j, t - 1].astype(F32)
        asend[j, t] = total.astype(BF)
        chain_a(j, t).start()
        if t < 3:
            total = own_sum(j, kb, 0, chunk)
            if t > 0:
                chain_b(j, t - 1).wait_recv()
                total = total + brecv[j, t - 1].astype(F32)
            bsend[j, t] = total.astype(BF)
            chain_b(j, t).start()

    mine = pl.ds(pl.multiple_of(SLOTS * me, SLOTS), SLOTS)

    def give_back(srcs, dst, send_sem, recv_sem):
        for core, src in enumerate(srcs):
            for i in range(blocks):
                b = c * blocks + i
                rows = pl.ds(SLOTS * i, SLOTS)
                own = jnp.logical_and(b == me, c == core)

                @pl.when(jnp.logical_not(own))
                def _():
                    remote(src.at[rows, :], dst.at[mine, :], send_sem, recv_sem, (z * 2 + core, b)).start()

                @pl.when(own)
                def _():
                    dst[mine, :] = src[rows, :]

    home = c == me // blocks

    def await_rows(ref, sem):
        @pl.when(home)
        def _():
            await_bytes(ref.at[pl.ds(0, SLOTS * (experts - 1)), :], sem)

        @pl.when(jnp.logical_not(home))
        def _():
            await_bytes(ref, sem)

    @jax.named_scope("chain_end")
    def chain_end(j):
        chain_a(j, 3).wait_recv()
        chain_b(j, 2).wait_recv()
        total = own_sum(j, 0, 0, chunk) + arecv[j, 3].astype(F32) + brecv[j, 2].astype(F32)
        ret_out[j] = total.astype(BF)
        give_back([ret_out.at[j]] * 2, ret.at[j], rs.at[j], rr.at[j])

    @jax.named_scope("late_back")
    def late_back(j):
        n = j - CHAINS
        for g in range(2):
            sib_p(j, g).wait_recv()
            total = (part[j, g, own_rows, :].astype(F32) + sib[j, g].astype(F32)).astype(BF)
            for i in range(NZ // 2):
                late_out[n, i, g] = total[:, chunk * i : chunk * (i + 1)]
        for i in range(NZ // 2):
            give_back([late_out.at[n, i, 0], late_out.at[n, i, 1]], late_in.at[n, i], rs.at[j], rl.at[n, i])

    own_toks = pl.ds(pl.multiple_of(htoks * c, htoks), htoks)

    @jax.named_scope("mix")
    def mix(j):
        await_rows(ret.at[j], rr.at[j])
        term = jnp.dot(chi[j], ret[j], preferred_element_type=F32)
        term = term + jnp.dot(clo[j], ret[j], preferred_element_type=F32)
        acc[...] = term if j == 0 else acc[...] + term

    def give(p, k):
        here = mixed.at[p, z, own_toks, :]
        return remote(here, here, os_.at[0], or_.at[p], zdev(k))

    def hand(p):
        here = mixed.at[p, :, own_toks, :]
        return remote(here, here, gs.at[0], gr.at[p], sibling)

    @jax.named_scope("late_mix")
    def late_mix(i):
        term = jnp.zeros((toks, chunk), F32)
        for n in range(BATCHES - CHAINS):
            await_rows(late_in.at[n, i], rl.at[n, i])
            term = term + jnp.dot(chi[CHAINS + n], late_in[n, i], preferred_element_type=F32)
            term = term + jnp.dot(clo[CHAINS + n], late_in[n, i], preferred_element_type=F32)
        zsend[i] = term.astype(BF)
        k = ORDER[0][i] * (1 - c) + ORDER[1][i] * c
        for core in range(2):
            copy = remote(
                zsend.at[i, pl.ds(htoks * core, htoks), :], zrecv.at[k], zs.at[0], zr.at[0], zdev(k, core))
            if ORDER[1][i] == 0 and core == 1:
                @pl.when(c == 0)
                def _():
                    copy.start()

                @pl.when(c == 1)
                def _():
                    zrecv[0] = zsend[i, htoks:, :]
            else:
                copy.start()

    def await_parts(ref, sem):
        @pl.when(c == 0)
        def _():
            await_bytes(ref, sem)

        @pl.when(c == 1)
        def _():
            await_bytes(ref.at[pl.ds(0, NZ - 1)], sem)

    @jax.named_scope("gather")
    def gather():
        await_parts(zrecv, zr.at[0])
        for p in range(PIECES):
            cols = slice(col * p, col * (p + 1))
            total = acc[own_toks, cols]
            for k in range(NZ):
                total = total + zrecv[k, :, cols].astype(F32)
            mixed[p, z, own_toks, :] = total.astype(BF)
            for k in (4, 3, 5, 2, 6, 1, 7):
                give(p, k).start()

    @jax.named_scope("take")
    def take(j):
        if j >= BATCHES:
            return
        await_bytes(xin.at[j, 0, pl.ds(0, SLOTS * SIDE * (SIDE - 1)), :], xr.at[j])
        if j + 2 < BATCHES:
            dispatch_all(j + 2)
        sib_x(j).start()

    @jax.named_scope("up")
    def up(j, h):
        gate = jnp.dot(xin[j, h], wg[h], preferred_element_type=F32)
        raised = jnp.dot(xin[j, h], wu[h], preferred_element_type=F32)
        if h == 0:
            gacc[...] = gate
            uacc[...] = raised
            return None
        gate = gacc[...] + gate
        raised = uacc[...] + raised
        return (gate / (1.0 + jnp.exp(-gate)) * raised).astype(BF)

    @jax.named_scope("down")
    def down(j, hidden):
        for g in range(2):
            part[j, g] = jnp.dot(hidden, wd[g], preferred_element_type=F32).astype(BF)
            sib_p(j, g).start()

    def after(j):
        if j < 0:
            return
        if j >= CHAINS:
            late_back(j)
        for t in range(4):
            chain_step(j - t, t)

    take(0)
    for j in range(BATCHES):
        if j == 0:
            loads[0].wait()
            loads[1].wait()
        up(j, 0)
        after(j - 1)
        if j == 0:
            loads[2].wait()
            loads[3].wait()
        with jax.named_scope("sib_wait"):
            sib_x(j).wait_recv()
        hidden = up(j, 1)
        if j == 0:
            await_bytes(wd, w_sem.at[4])
        take(j + 1)
        down(j, hidden)
    after(BATCHES - 1)
    chain_step(1, 3)
    chain_end(0)
    late_mix(0)
    chain_end(1)
    late_mix(1)
    late_mix(2)
    late_mix(3)
    mix(0)
    mix(1)
    gather()

    with jax.named_scope("drain"):
        await_bytes(slots.at[:, pl.ds(0, SIDE - 1)], ns.at[0])
        await_bytes(line.at[:, :, pl.ds(0, SIDE - 1)], ls.at[0])
        await_bytes(packed.at[:, :, pl.ds(0, SIDE - 1)], xs.at[0])
        await_bytes(xin.at[:, 0], fs.at[0])
        await_bytes(part.at[:, :, pl.ds(0, hrows), :], ps.at[0])
        await_bytes(asend, as_.at[0])
        await_bytes(bsend, bs.at[0])
        for j in range(CHAINS):
            await_rows(ret.at[j], rs.at[j])
        for n in range(BATCHES - CHAINS):
            for i in range(NZ // 2):
                await_rows(late_in.at[n, i], rs.at[CHAINS + n])
        await_parts(zrecv, zs.at[0])

    for p in range(PIECES):
        with jax.named_scope("gather_wait"):
            await_bytes(mixed.at[p, pl.ds(0, NZ - 1), pl.ds(0, htoks), :], or_.at[p])
        hand(p).start()
    for p in range(PIECES):
        with jax.named_scope("hand_wait"):
            hand(p).wait_recv()
        for k in range(NZ):
            out[:, chunk * k + col * p : chunk * k + col * (p + 1)] = mixed[p, k]
    await_bytes(mixed.at[:, pl.ds(0, NZ - 1), pl.ds(0, htoks), :], os_.at[0])
    await_bytes(mixed.at[:, :, pl.ds(0, htoks), :], gs.at[0])


def on_device(tokens, norm_gain, expert_ids, gates, gate_proj, up_proj, down_proj):
    toks, features = tokens.shape
    experts = lax.axis_size("expert")
    width = gate_proj.shape[2]
    half, chunk = features // 2, features // NZ
    fine, col = half // (2 * PARTS), chunk // PIECES
    rows = experts * SLOTS
    hrows = rows // 2
    dma = pltpu.SemaphoreType.DMA
    vmem = pl.BlockSpec(memory_space=pltpu.VMEM)
    hbm = pl.BlockSpec(memory_space=pl.ANY)
    b = BATCHES
    scratch = [
        pltpu.VMEM((2, half, width), BF),
        pltpu.VMEM((2, half, width), BF),
        pltpu.VMEM((2, width, half), BF),
        pltpu.VMEM((2, PARTS, SIDE, toks, fine), BF),
        pltpu.VMEM((2, SIDE, experts, toks), F32),
        pltpu.VMEM((b, toks, rows), BF),
        pltpu.VMEM((b, toks, rows), BF),
        pltpu.VMEM((b, 2, SIDE, SIDE, SLOTS, half // 2), BF),
        pltpu.VMEM((b, 2, rows, half), BF),
        pltpu.VMEM((rows, width), F32),
        pltpu.VMEM((rows, width), F32),
        pltpu.VMEM((b, 2, rows, half), BF),
        pltpu.VMEM((b, 2, hrows, half), BF),
        pltpu.VMEM((CHAINS, 4, hrows, chunk), BF),
        pltpu.VMEM((CHAINS, 4, hrows, chunk), BF),
        pltpu.VMEM((CHAINS, 3, hrows, chunk), BF),
        pltpu.VMEM((CHAINS, 3, hrows, chunk), BF),
        pltpu.VMEM((CHAINS, hrows, chunk), BF),
        pltpu.VMEM((CHAINS, rows, chunk), BF),
        pltpu.VMEM((b - CHAINS, NZ // 2, 2, hrows, chunk), BF),
        pltpu.VMEM((b - CHAINS, NZ // 2, rows, chunk), BF),
        pltpu.VMEM((NZ // 2, toks, chunk), BF),
        pltpu.VMEM((NZ, toks // 2, chunk), BF),
        pltpu.VMEM((toks, chunk), F32),
        pltpu.VMEM((PIECES, NZ, toks, col), BF),
        dma((5,)),
        dma((1,)), dma((2, PARTS)),
        dma((1,)), dma((2,)),
        dma((1,)), dma((b,)),
        dma((1,)), dma((b,)),
        dma((1,)), dma((b, 2)),
        dma((1,)), dma((CHAINS, 4)),
        dma((1,)), dma((CHAINS, 3)),
        dma((b,)), dma((CHAINS,)), dma((b - CHAINS, NZ // 2)),
        dma((1,)), dma((1,)),
        dma((1,)), dma((PIECES,)),
        dma((1,)), dma((PIECES,)),
    ]
    return pl.pallas_call(
        kernel,
        out_shape=pltpu.VMEM((toks, features), BF),
        in_specs=[vmem, vmem, vmem, vmem, hbm, hbm, hbm],
        out_specs=vmem,
        scratch_shapes=scratch,
        compiler_params=pltpu.CompilerParams(
            collective_id=0, has_side_effects=True, vmem_limit_bytes=60 << 20
        ),
    )(tokens, norm_gain.reshape(1, -1), expert_ids.T, gates.T, gate_proj, up_proj, down_proj)


def solution(mesh):
    return jax.shard_map(
        on_device,
        mesh=mesh,
        in_specs=(
            P("expert", None),
            P(),
            P("expert", None),
            P("expert", None),
            P("expert", None, "section"),
            P("expert", None, "section"),
            P("expert", "section", None),
        ),
        out_specs=P("expert", None),
        check_vma=False,
    )
```

```python
import jax
import jax.numpy as jnp
from jax import lax
from jax.experimental import pallas as pl
from jax.experimental.pallas import tpu as pltpu
from jax.sharding import PartitionSpec as P

MESH = pl.DeviceIdType.MESH
BATCHES = 4
CHAINS = (0, 2)
LATE = (1, 3)
SLOTS = 16
NZ = 8
SIDE = 4
XY = [(dx, dy) for dx in range(SIDE) for dy in range(SIDE) if (dx, dy) != (0, 0)]
ORDER = ((4, 3, 5, 0), (2, 6, 1, 7))
STAGES = ((0, 3), (3, 4))
PLACE = {k: (g, i) for g, ks in enumerate(ORDER) for i, k in enumerate(ks)}
PIECES = 3
PARTS = 2
BF = jnp.bfloat16
F32 = jnp.float32


def kernel(
    tok_hbm, gain, ids, gates, wg_hbm, wu_hbm, wd_hbm, out,
    tok, wg, wu, wd, line, slots, chi, clo, packed, xin, gacc, uacc, part, sib,
    asend, arecv, bsend, brecv, ret_out, ret, late_out, late_in, zsend, zrecv, relay, acc, mixed,
    w_sem, ls, lr, ns, nr, xs, xr, fs, fr, ps, pr, as_, ar, bs, br, rs, rr, rl, zs, zr, zq, os_, or_, gs, gr,
):
    sec, me = lax.axis_index("section"), lax.axis_index("expert")
    z, c = sec // 2, sec % 2
    x, y = me // SIDE, me % SIDE
    experts = SIDE * SIDE
    blocks = experts // 2
    toks = tok.shape[0]
    htoks = toks // 2
    fine = line.shape[4]
    wide = fine * PARTS
    half = 2 * wide
    col = mixed.shape[3]
    chunk = col * PIECES
    hrows = blocks * SLOTS
    first_at, then_at = (x, y), (y, x)

    def on_first(f, i):
        return i * SIDE + y if f == 0 else x * SIDE + i

    def on_then(f, q):
        return x * SIDE + q if f == 0 else q * SIDE + y

    def zdev(dz, core=c):
        return (lax.rem(z + dz + 2 * NZ, NZ) * 2 + core, me)

    def xydev(dx, dy):
        return lax.rem(x + dx, SIDE) * SIDE + lax.rem(y + dy, SIDE)

    other = z * 2 + 1 - c
    sibling = (other, me)

    token_load = pltpu.make_async_copy(tok_hbm, tok, w_sem.at[5])
    token_load.start()

    barrier = pltpu.get_barrier_semaphore()
    for dx, dy in XY:
        for s in (sec, other):
            pl.semaphore_signal(barrier, inc=1, device_id=(s, xydev(dx, dy)), device_id_type=MESH)
    pl.semaphore_signal(barrier, inc=1, device_id=sibling, device_id_type=MESH)
    for k in range(1, NZ):
        for core in range(2):
            pl.semaphore_signal(barrier, inc=1, device_id=zdev(k, core), device_id_type=MESH)

    loads = []
    for h in range(2):
        lines = pl.ds(pl.multiple_of(half * lax.rem(c + h, 2), half), half)
        loads.append(pltpu.make_async_copy(wg_hbm.at[0, lines, :], wg.at[h], w_sem.at[2 * h]))
        loads.append(pltpu.make_async_copy(wu_hbm.at[0, lines, :], wu.at[h], w_sem.at[2 * h + 1]))
    for load in loads:
        load.start()
    for k in range(NZ):
        cols = pl.ds(pl.multiple_of(chunk * lax.rem(z + k, NZ), chunk), chunk)
        g, i = PLACE[k]
        pltpu.make_async_copy(wd_hbm.at[0, :, cols], wd.at[g, :, pl.ds(chunk * i, chunk)], w_sem.at[4]).start()

    def await_bytes(ref, sem):
        pltpu.make_async_copy(ref, ref, sem).wait()

    e_iota = lax.broadcasted_iota(jnp.int32, (experts, toks), 0)
    named = jnp.zeros((experts, toks), jnp.bool_)
    weight = jnp.zeros((experts, toks), F32)
    for k in range(ids.shape[0]):
        hit = e_iota == ids[k : k + 1, :]
        named = named | hit
        weight = weight + jnp.where(hit, gates[k : k + 1, :], 0.0)
    earlier = lax.broadcasted_iota(jnp.int32, (toks, toks), 0) < lax.broadcasted_iota(jnp.int32, (toks, toks), 1)
    slot = jnp.dot(
        jnp.where(named, 1.0, 0.0).astype(BF), jnp.where(earlier, 1.0, 0.0).astype(BF), preferred_element_type=F32)
    slot = jnp.where(named, slot, -1.0)
    for f in range(2):
        slots[f, first_at[f]] = slot

    with jax.named_scope("norm"):
        token_load.wait()
        values = tok[...].astype(F32)
        average = jnp.mean(values, axis=-1, keepdims=True)
        centered = values - average
        variance = jnp.mean(centered * centered, axis=-1, keepdims=True)
        scale = lax.rsqrt(variance + 1e-05)
        for f in range(2):
            for s in range(PARTS):
                cols = pl.ds(pl.multiple_of(half * c + wide * f + fine * s, fine), fine)
                part_values = tok[:, cols].astype(F32) - average
                line[f, s, first_at[f]] = (part_values * scale * gain[:, cols]).astype(BF)

    def remote(src, dst, send_sem, recv_sem, to):
        return pltpu.make_async_remote_copy(
            src_ref=src, dst_ref=dst, send_sem=send_sem, recv_sem=recv_sem, device_id=to, device_id_type=MESH)

    with jax.named_scope("entry_wait"):
        pl.semaphore_wait(barrier, 2 * len(XY) + 2 * NZ - 1)
    def mates(f):
        return [(sec, on_first(f, lax.rem(first_at[f] + k, SIDE))) for k in (1, 3, 2)]

    for f in range(2):
        for to in mates(f):
            here = slots.at[f, first_at[f]]
            remote(here, here, ns.at[0], nr.at[f], to).start()
    for s in range(PARTS):
        for f in range(2):
            for to in mates(f):
                here = line.at[f, s, first_at[f]]
                remote(here, here, ls.at[0], lr.at[f, s], to).start()

    def shares(low, count, hi, lo):
        places = lax.broadcasted_iota(jnp.int32, (count, toks), 0).astype(F32) + float(low)
        rows = [jnp.where(slot[e : e + 1, :] == places, weight[e : e + 1, :], 0.0) for e in range(experts)]
        share = jnp.transpose(jnp.concatenate(rows, axis=0))
        top = share.astype(BF)
        hi[...] = top
        lo[...] = (share - top.astype(F32)).astype(BF)

    with jax.named_scope("shares"):
        for j in range(BATCHES):
            shares(SLOTS * j, SLOTS, chi.at[j], clo.at[j])

    def block_rows(f, i):
        return pl.ds(pl.multiple_of(SLOTS * on_first(f, i), SLOTS), SLOTS)

    s_iota = lax.broadcasted_iota(jnp.int32, (SLOTS, toks), 0).astype(F32)

    def picks(js, f, i):
        rows = []
        for j in js:
            for q in range(SIDE):
                row = slots[f, i, pl.ds(on_then(f, q), 1), :]
                rows.append(jnp.where((row - float(SLOTS * j)) == s_iota, 1.0, 0.0).astype(BF))
        return jnp.concatenate(rows, axis=0)

    @jax.named_scope("pack")
    def pack(js, f, parts):
        for i in range(SIDE):
            chosen = picks(js, f, i)
            for s in parts:
                cols = slice(fine * s, fine * (s + 1))
                rows = jnp.dot(chosen, line[f, s, i], preferred_element_type=F32).astype(BF)
                for n, j in enumerate(js):
                    for q in range(SIDE):
                        at = SLOTS * (n * SIDE + q)
                        packed[j, f, q, i, :, cols] = rows[at : at + SLOTS, :]
        for j in js:
            for i in range(SIDE):
                for s in parts:
                    cols = slice(fine * s, fine * (s + 1))
                    to = slice(wide * f + fine * s, wide * f + fine * (s + 1))
                    xin[j, 0, block_rows(f, i), to] = packed[j, f, then_at[f], i, :, cols]

    def dispatch(j, f, first, count):
        for k in (1, 3, 2):
            q = lax.rem(then_at[f] + k, SIDE)
            for i in range(SIDE):
                remote(
                    packed.at[j, f, q, i, :, pl.ds(first, count)],
                    xin.at[j, 0, block_rows(f, i), pl.ds(wide * f + first, count)], xs.at[0], xr.at[j],
                    (sec, on_then(f, q))).start()

    for f in range(2):
        await_bytes(slots.at[f, pl.ds(0, SIDE - 1)], nr.at[f])
    for s in range(PARTS):
        for f in range(2):
            with jax.named_scope("line_wait"):
                await_bytes(line.at[f, s, pl.ds(0, SIDE - 1)], lr.at[f, s])
            pack([0], f, [s])
            dispatch(0, f, fine * s, fine)

    def dispatch_all(j):
        for f in range(2):
            dispatch(j, f, 0, wide)

    for f in range(2):
        pack(list(range(1, BATCHES)), f, range(PARTS))
    dispatch_all(1)

    def sib_x(j):
        return remote(xin.at[j, 0], xin.at[j, 1], fs.at[0], fr.at[j], sibling)

    own_rows = pl.ds(pl.multiple_of(hrows * c, hrows), hrows)
    sib_rows = pl.ds(pl.multiple_of(hrows * (1 - c), hrows), hrows)

    def sib_p(j, g):
        return remote(part.at[j, g, sib_rows, :], sib.at[j, g], ps.at[0], pr.at[j, g], sibling)

    def own_sum(j, k, first, count):
        g, i = PLACE[k % NZ]
        cols = slice(chunk * i + first, chunk * i + first + count)
        return part[j, g, own_rows, cols].astype(F32) + sib[j, g, :, cols].astype(F32)

    def sign(u):
        return 1 - 2 * (u % 2)

    def chain_a(u, t, p):
        return remote(asend.at[u, t, p], arecv.at[u, t, p], as_.at[0], ar.at[u, t, p], zdev(-sign(u)))

    def chain_b(u, t, p):
        return remote(bsend.at[u, t, p], brecv.at[u, t, p], bs.at[0], br.at[u, t, p], zdev(sign(u)))

    @jax.named_scope("chain_step")
    def chain_step(u, t):
        j = CHAINS[u]
        ka, kb = 4 + sign(u) * t, 4 - sign(u) * (1 + t)
        if t < 2:
            sib_p(j, t).wait_recv()
        for p in range(PIECES):
            total = own_sum(j, ka, col * p, col)
            if t > 0:
                chain_a(u, t - 1, p).wait_recv()
                total = total + arecv[u, t - 1, p].astype(F32)
            asend[u, t, p] = total.astype(BF)
            chain_a(u, t, p).start()
            if t < 3:
                total = own_sum(j, kb, col * p, col)
                if t > 0:
                    chain_b(u, t - 1, p).wait_recv()
                    total = total + brecv[u, t - 1, p].astype(F32)
                bsend[u, t, p] = total.astype(BF)
                chain_b(u, t, p).start()

    mine = pl.ds(pl.multiple_of(SLOTS * me, SLOTS), SLOTS)

    def give_back(srcs, dst, send_sem, recv_sem):
        for core, src in enumerate(srcs):
            for i in range(blocks):
                b = c * blocks + i
                rows = pl.ds(SLOTS * i, SLOTS)
                own = jnp.logical_and(b == me, c == core)

                @pl.when(jnp.logical_not(own))
                def _():
                    remote(src.at[rows, :], dst.at[mine, :], send_sem, recv_sem, (z * 2 + core, b)).start()

                @pl.when(own)
                def _():
                    dst[mine, :] = src[rows, :]

    home = c == me // blocks

    def await_rows(ref, sem):
        @pl.when(home)
        def _():
            await_bytes(ref.at[pl.ds(0, SLOTS * (experts - 1)), :], sem)

        @pl.when(jnp.logical_not(home))
        def _():
            await_bytes(ref, sem)

    @jax.named_scope("chain_end")
    def chain_end(u):
        for p in range(PIECES):
            chain_a(u, 3, p).wait_recv()
            chain_b(u, 2, p).wait_recv()
            total = own_sum(CHAINS[u], 0, col * p, col) + arecv[u, 3, p].astype(F32) + brecv[u, 2, p].astype(F32)
            ret_out[u, :, col * p : col * (p + 1)] = total.astype(BF)
        give_back([ret_out.at[u]] * 2, ret.at[u], rs.at[CHAINS[u]], rr.at[u])

    @jax.named_scope("late_back")
    def late_back(n):
        j = LATE[n]
        for g in range(2):
            sib_p(j, g).wait_recv()
            for h, (i0, i1) in enumerate(STAGES):
                cols = slice(chunk * i0, chunk * i1)
                total = part[j, g, own_rows, cols].astype(F32) + sib[j, g, :, cols].astype(F32)
                late_out[n, g, :, cols] = total.astype(BF)
        for h, (i0, i1) in enumerate(STAGES):
            cols = pl.ds(chunk * i0, chunk * (i1 - i0))
            give_back(
                [late_out.at[n, g, :, cols] for g in range(2)], late_in.at[n, :, cols], rs.at[j], rl.at[n, h])

    own_toks = pl.ds(pl.multiple_of(htoks * c, htoks), htoks)

    @jax.named_scope("mix")
    def mix(u):
        await_rows(ret.at[u], rr.at[u])
        term = jnp.dot(chi[CHAINS[u]], ret[u], preferred_element_type=F32)
        term = term + jnp.dot(clo[CHAINS[u]], ret[u], preferred_element_type=F32)
        acc[...] = term if u == 0 else acc[...] + term

    def give(p, at, k, first, count, sem):
        here = mixed.at[p, lax.rem(z + at + NZ, NZ), pl.ds(pl.multiple_of(htoks * c, htoks) + first, count), :]
        return remote(here, here, os_.at[0], or_.at[p, sem], zdev(k))

    def pass_on(p):
        for side in (1, -1):
            await_bytes(mixed.at[p, 0, pl.ds(0, htoks), :], or_.at[p, (1 - side) // 2])
            give(p, -2 * side, side, 0, htoks, 2).start()
            give(p, -2 * side, 2 * side, htoks // 4 * (1 - side), htoks // 2, 2).start()

    def hand(p):
        here = mixed.at[p, :, own_toks, :]
        return remote(here, here, gs.at[0], gr.at[p], sibling)

    @jax.named_scope("late_mix")
    def late_mix(h):
        i0, i1 = STAGES[h]
        cols = slice(chunk * i0, chunk * i1)
        term = jnp.zeros((toks, chunk * (i1 - i0)), F32)
        for n, j in enumerate(LATE):
            await_rows(late_in.at[n, :, pl.ds(chunk * i0, chunk * (i1 - i0))], rl.at[n, h])
            term = term + jnp.dot(chi[j], late_in[n, :, cols], preferred_element_type=F32)
            term = term + jnp.dot(clo[j], late_in[n, :, cols], preferred_element_type=F32)
        for i in range(i0, i1):
            zsend[i] = term[:, chunk * (i - i0) : chunk * (i - i0 + 1)].astype(BF)
        low, high = pl.ds(0, htoks), pl.ds(htoks, htoks)

        @pl.when(c == 0)
        def _():
            if h == 0:
                relay_send(zsend.at[0, low, :], 0, pl.ds(toks, htoks), 2)
                relay_send(zsend.at[0, high, :], 1, pl.ds(toks, htoks), -2)
                relay_send(zsend.at[1], 0, pl.ds(0, toks), 1)
                relay_send(zsend.at[2], 1, pl.ds(0, toks), -1)
            else:
                zrecv[0] = zsend[3, :htoks, :]
                remote(zsend.at[3, high, :], zrecv.at[0], zs.at[0], zr.at[0], sibling).start()

        @pl.when(c == 1)
        def _():
            owner_send(2 + h, 1 + h, 1 - 2 * h)

    def relay_send(src, side, rows, k):
        remote(src, relay.at[side, rows, :], zs.at[0], zq.at[0], zdev(k, 1)).start()

    def owner_send(i, n, k):
        for core in range(2):
            remote(zsend.at[i, pl.ds(htoks * core, htoks), :], zrecv.at[n], zs.at[0], zr.at[0], zdev(k, core)).start()

    @jax.named_scope("relay_sum")
    def relay_sum():
        @pl.when(c == 1)
        def _():
            await_bytes(relay, zq.at[0])
            for side in range(2):
                total = zsend[side].astype(F32) + relay[side, :toks, :].astype(F32)
                far = slice(htoks * side, htoks * (side + 1))
                near = slice(htoks * (1 - side), htoks * (2 - side))
                zsend[side, near, :] = total[near, :].astype(BF)
                zsend[side, far, :] = (total[far, :] + relay[side, toks:, :].astype(F32)).astype(BF)
                owner_send(side, 3 + side, 2 - 4 * side)

    def await_parts(ref, sem):
        @pl.when(c == 1)
        def _():
            await_bytes(ref, sem)

        @pl.when(c == 0)
        def _():
            await_bytes(ref.at[pl.ds(0, 4)], sem)

    @jax.named_scope("gather")
    def gather():
        await_parts(zrecv, zr.at[0])
        for p in range(PIECES):
            cols = slice(col * p, col * (p + 1))
            total = acc[own_toks, cols]
            for k in range(5):
                total = total + zrecv[k, :, cols].astype(F32)
            mixed[p, z, own_toks, :] = total.astype(BF)
            for k in (2, -2, 1, -1):
                give(p, 0, k, 0, htoks, {2: 0, -2: 1, 1: 2, -1: 2}[k]).start()

    @jax.named_scope("take")
    def take(j):
        if j >= BATCHES:
            return
        await_bytes(xin.at[j, 0, pl.ds(0, SLOTS * SIDE * (SIDE - 1)), :], xr.at[j])
        if j + 2 < BATCHES:
            dispatch_all(j + 2)
        sib_x(j).start()

    @jax.named_scope("up")
    def up(j, h):
        gate = jnp.dot(xin[j, h], wg[h], preferred_element_type=F32)
        raised = jnp.dot(xin[j, h], wu[h], preferred_element_type=F32)
        if h == 0:
            gacc[...] = gate
            uacc[...] = raised
            return None
        gate = gacc[...] + gate
        raised = uacc[...] + raised
        return (gate / (1.0 + jnp.exp(-gate)) * raised).astype(BF)

    @jax.named_scope("down")
    def down(j, hidden):
        for g in range(2):
            part[j, g] = jnp.dot(hidden, wd[g], preferred_element_type=F32).astype(BF)
            sib_p(j, g).start()

    def after(j):
        if j == 0:
            chain_step(0, 0)
        if j == 1:
            late_back(0)
            chain_step(0, 1)
        if j == 2:
            chain_step(1, 0)
        if j == 3:
            chain_step(0, 2)
            chain_step(1, 1)
            late_back(1)

    take(0)
    for j in range(BATCHES):
        if j == 0:
            loads[0].wait()
            loads[1].wait()
        up(j, 0)
        after(j - 1)
        if j == 0:
            loads[2].wait()
            loads[3].wait()
        with jax.named_scope("sib_wait"):
            sib_x(j).wait_recv()
        hidden = up(j, 1)
        if j == 0:
            await_bytes(wd, w_sem.at[4])
        if j > 0:
            take(j + 1)
        down(j, hidden)
        if j == 0:
            take(1)
    after(BATCHES - 1)
    chain_step(1, 2)
    chain_step(0, 3)
    chain_step(1, 3)
    late_mix(0)
    chain_end(1)
    chain_end(0)
    late_mix(1)
    relay_sum()
    mix(0)
    mix(1)
    gather()

    with jax.named_scope("drain"):
        await_bytes(slots.at[:, pl.ds(0, SIDE - 1)], ns.at[0])
        await_bytes(line.at[:, :, pl.ds(0, SIDE - 1)], ls.at[0])
        await_bytes(packed.at[:, :, pl.ds(0, SIDE - 1)], xs.at[0])
        await_bytes(xin.at[:, 0], fs.at[0])
        await_bytes(part.at[:, :, pl.ds(0, hrows), :], ps.at[0])
        await_bytes(asend, as_.at[0])
        await_bytes(bsend, bs.at[0])
        for u, j in enumerate(CHAINS):
            await_rows(ret.at[u], rs.at[j])
        for n, j in enumerate(LATE):
            await_rows(late_in.at[n], rs.at[j])
        @pl.when(c == 0)
        def _():
            await_bytes(late_in.at[0, pl.ds(0, 7 * htoks * chunk // half), :], zs.at[0])

        @pl.when(c == 1)
        def _():
            await_bytes(zsend, zs.at[0])

    for p in range(PIECES):
        with jax.named_scope("pass_on"):
            pass_on(p)
    for p in range(PIECES):
        with jax.named_scope("gather_wait"):
            await_bytes(mixed.at[p, pl.ds(0, NZ - 3), pl.ds(0, htoks), :], or_.at[p, 2])
        hand(p).start()
    for p in range(PIECES):
        with jax.named_scope("hand_wait"):
            hand(p).wait_recv()
        for k in range(NZ):
            out[:, chunk * k + col * p : chunk * k + col * (p + 1)] = mixed[p, k]
    await_bytes(mixed.at[:, pl.ds(0, NZ - 1), pl.ds(0, htoks), :], os_.at[0])
    await_bytes(mixed.at[:, :, pl.ds(0, htoks), :], gs.at[0])


def on_device(tokens, norm_gain, expert_ids, gates, gate_proj, up_proj, down_proj):
    toks, features = tokens.shape
    experts = lax.axis_size("expert")
    width = gate_proj.shape[2]
    half, chunk = features // 2, features // NZ
    fine, col = half // (2 * PARTS), chunk // PIECES
    rows = experts * SLOTS
    hrows = rows // 2
    dma = pltpu.SemaphoreType.DMA
    vmem = pl.BlockSpec(memory_space=pltpu.VMEM)
    hbm = pl.BlockSpec(memory_space=pl.ANY)
    b = BATCHES
    scratch = [
        pltpu.VMEM((toks, features), BF),
        pltpu.VMEM((2, half, width), BF),
        pltpu.VMEM((2, half, width), BF),
        pltpu.VMEM((2, width, half), BF),
        pltpu.VMEM((2, PARTS, SIDE, toks, fine), BF),
        pltpu.VMEM((2, SIDE, experts, toks), F32),
        pltpu.VMEM((b, toks, rows), BF),
        pltpu.VMEM((b, toks, rows), BF),
        pltpu.VMEM((b, 2, SIDE, SIDE, SLOTS, half // 2), BF),
        pltpu.VMEM((b, 2, rows, half), BF),
        pltpu.VMEM((rows, width), F32),
        pltpu.VMEM((rows, width), F32),
        pltpu.VMEM((b, 2, rows, half), BF),
        pltpu.VMEM((b, 2, hrows, half), BF),
        pltpu.VMEM((len(CHAINS), 4, PIECES, hrows, col), BF),
        pltpu.VMEM((len(CHAINS), 4, PIECES, hrows, col), BF),
        pltpu.VMEM((len(CHAINS), 3, PIECES, hrows, col), BF),
        pltpu.VMEM((len(CHAINS), 3, PIECES, hrows, col), BF),
        pltpu.VMEM((len(CHAINS), hrows, chunk), BF),
        pltpu.VMEM((len(CHAINS), rows, chunk), BF),
        pltpu.VMEM((len(LATE), 2, hrows, half), BF),
        pltpu.VMEM((len(LATE), rows, half), BF),
        pltpu.VMEM((NZ // 2, toks, chunk), BF),
        pltpu.VMEM((5, toks // 2, chunk), BF),
        pltpu.VMEM((2, toks + toks // 2, chunk), BF),
        pltpu.VMEM((toks, chunk), F32),
        pltpu.VMEM((PIECES, NZ, toks, col), BF),
        dma((6,)),
        dma((1,)), dma((2, PARTS)),
        dma((1,)), dma((2,)),
        dma((1,)), dma((b,)),
        dma((1,)), dma((b,)),
        dma((1,)), dma((b, 2)),
        dma((1,)), dma((len(CHAINS), 4, PIECES)),
        dma((1,)), dma((len(CHAINS), 3, PIECES)),
        dma((b,)), dma((len(CHAINS),)), dma((len(LATE), len(STAGES))),
        dma((1,)), dma((1,)), dma((1,)),
        dma((1,)), dma((PIECES, 3)),
        dma((1,)), dma((PIECES,)),
    ]
    return pl.pallas_call(
        kernel,
        out_shape=pltpu.VMEM((toks, features), BF),
        in_specs=[hbm, vmem, vmem, vmem, hbm, hbm, hbm],
        out_specs=vmem,
        scratch_shapes=scratch,
        compiler_params=pltpu.CompilerParams(
            collective_id=0, has_side_effects=True, vmem_limit_bytes=60 << 20
        ),
    )(tokens, norm_gain.reshape(1, -1), expert_ids.T, gates.T, gate_proj, up_proj, down_proj)


def solution(mesh):
    return jax.shard_map(
        on_device,
        mesh=mesh,
        in_specs=(
            P("expert", None),
            P(),
            P("expert", None),
            P("expert", None),
            P("expert", None, "section"),
            P("expert", None, "section"),
            P("expert", "section", None),
        ),
        out_specs=P("expert", None),
        check_vma=False,
    )
```

```python
import jax
import jax.numpy as jnp
from jax import lax
from jax.experimental import pallas as pl
from jax.experimental.pallas import tpu as pltpu
from jax.sharding import PartitionSpec as P

MESH = pl.DeviceIdType.MESH
BATCHES = 4
CHAINS = (0, 2)
LATE = (1, 3)
SLOTS = 16
NZ = 8
SIDE = 4
XY = [(dx, dy) for dx in range(SIDE) for dy in range(SIDE) if (dx, dy) != (0, 0)]
ORDER = ((4, 3, 5, 0), (2, 6, 1, 7))
STAGES = ((0, 3), (3, 4))
PLACE = {k: (g, i) for g, ks in enumerate(ORDER) for i, k in enumerate(ks)}
PIECES = 3
PARTS = 2
BF = jnp.bfloat16
F32 = jnp.float32


def kernel(
    tok_hbm, gain, ids, gates, wg_hbm, wu_hbm, wd_hbm, out,
    tok, wg, wu, wd, line, slots, chi, clo, packed, xin, gacc, uacc, part, sib,
    asend, arecv, bsend, brecv, ret_out, ret, late_out, late_in, zsend, zrecv, relay, acc, mixed,
    w_sem, ls, lr, ns, nr, xs, xr, fs, fr, ps, pr, as_, ar, bs, br, rs, rr, rl, zs, zr, zq, os_, or_, gs, gr,
):
    sec, me = lax.axis_index("section"), lax.axis_index("expert")
    z, c = sec // 2, sec % 2
    x, y = me // SIDE, me % SIDE
    experts = SIDE * SIDE
    blocks = experts // 2
    toks = tok.shape[0]
    htoks = toks // 2
    fine = line.shape[4]
    wide = fine * PARTS
    half = 2 * wide
    col = mixed.shape[3]
    chunk = col * PIECES
    hrows = blocks * SLOTS
    first_at, then_at = (x, y), (y, x)

    def on_first(f, i):
        return i * SIDE + y if f == 0 else x * SIDE + i

    def on_then(f, q):
        return x * SIDE + q if f == 0 else q * SIDE + y

    def zdev(dz, core=c):
        return (lax.rem(z + dz + 2 * NZ, NZ) * 2 + core, me)

    def xydev(dx, dy):
        return lax.rem(x + dx, SIDE) * SIDE + lax.rem(y + dy, SIDE)

    other = z * 2 + 1 - c
    sibling = (other, me)

    token_load = pltpu.make_async_copy(tok_hbm, tok, w_sem.at[5])
    token_load.start()

    barrier = pltpu.get_barrier_semaphore()
    for dx, dy in XY:
        for s in (sec, other):
            pl.semaphore_signal(barrier, inc=1, device_id=(s, xydev(dx, dy)), device_id_type=MESH)
    pl.semaphore_signal(barrier, inc=1, device_id=sibling, device_id_type=MESH)
    for k in range(1, NZ):
        for core in range(2):
            pl.semaphore_signal(barrier, inc=1, device_id=zdev(k, core), device_id_type=MESH)

    loads = []
    for h in range(2):
        lines = pl.ds(pl.multiple_of(half * lax.rem(c + h, 2), half), half)
        loads.append(pltpu.make_async_copy(wg_hbm.at[0, lines, :], wg.at[h], w_sem.at[2 * h]))
        loads.append(pltpu.make_async_copy(wu_hbm.at[0, lines, :], wu.at[h], w_sem.at[2 * h + 1]))
    for load in loads:
        load.start()
    for k in range(NZ):
        cols = pl.ds(pl.multiple_of(chunk * lax.rem(z + k, NZ), chunk), chunk)
        g, i = PLACE[k]
        pltpu.make_async_copy(wd_hbm.at[0, :, cols], wd.at[g, :, pl.ds(chunk * i, chunk)], w_sem.at[4]).start()

    def await_bytes(ref, sem):
        pltpu.make_async_copy(ref, ref, sem).wait()

    e_iota = lax.broadcasted_iota(jnp.int32, (experts, toks), 0)
    named = jnp.zeros((experts, toks), jnp.bool_)
    weight = jnp.zeros((experts, toks), F32)
    for k in range(ids.shape[0]):
        hit = e_iota == ids[k : k + 1, :]
        named = named | hit
        weight = weight + jnp.where(hit, gates[k : k + 1, :], 0.0)
    earlier = lax.broadcasted_iota(jnp.int32, (toks, toks), 0) < lax.broadcasted_iota(jnp.int32, (toks, toks), 1)
    slot = jnp.dot(
        jnp.where(named, 1.0, 0.0).astype(BF), jnp.where(earlier, 1.0, 0.0).astype(BF), preferred_element_type=F32)
    slot = jnp.where(named, slot, -1.0)
    for f in range(2):
        slots[f, first_at[f]] = slot

    with jax.named_scope("norm"):
        token_load.wait()
        values = tok[...].astype(F32)
        average = jnp.mean(values, axis=-1, keepdims=True)
        centered = values - average
        variance = jnp.mean(centered * centered, axis=-1, keepdims=True)
        scale = lax.rsqrt(variance + 1e-05)
        for f in range(2):
            for s in range(PARTS):
                cols = pl.ds(pl.multiple_of(half * c + wide * f + fine * s, fine), fine)
                part_values = tok[:, cols].astype(F32) - average
                line[f, s, first_at[f]] = (part_values * scale * gain[:, cols]).astype(BF)

    def remote(src, dst, send_sem, recv_sem, to):
        return pltpu.make_async_remote_copy(
            src_ref=src, dst_ref=dst, send_sem=send_sem, recv_sem=recv_sem, device_id=to, device_id_type=MESH)

    with jax.named_scope("entry_wait"):
        pl.semaphore_wait(barrier, 2 * len(XY) + 2 * NZ - 1)
    def mates(f):
        return [(sec, on_first(f, lax.rem(first_at[f] + k, SIDE))) for k in (1, 3, 2)]

    for f in range(2):
        for to in mates(f):
            here = slots.at[f, first_at[f]]
            remote(here, here, ns.at[0], nr.at[f], to).start()
    for s in range(PARTS):
        for f in range(2):
            for to in mates(f):
                here = line.at[f, s, first_at[f]]
                remote(here, here, ls.at[0], lr.at[f, s], to).start()

    def shares(low, count, hi, lo):
        places = lax.broadcasted_iota(jnp.int32, (count, toks), 0).astype(F32) + float(low)
        rows = [jnp.where(slot[e : e + 1, :] == places, weight[e : e + 1, :], 0.0) for e in range(experts)]
        share = jnp.transpose(jnp.concatenate(rows, axis=0))
        top = share.astype(BF)
        hi[...] = top
        lo[...] = (share - top.astype(F32)).astype(BF)

    with jax.named_scope("shares"):
        for j in range(BATCHES):
            shares(SLOTS * j, SLOTS, chi.at[j], clo.at[j])

    def block_rows(f, i):
        return pl.ds(pl.multiple_of(SLOTS * on_first(f, i), SLOTS), SLOTS)

    s_iota = lax.broadcasted_iota(jnp.int32, (SLOTS, toks), 0).astype(F32)

    def picks(js, f, i):
        rows = []
        for j in js:
            for q in range(SIDE):
                row = slots[f, i, pl.ds(on_then(f, q), 1), :]
                rows.append(jnp.where((row - float(SLOTS * j)) == s_iota, 1.0, 0.0).astype(BF))
        return jnp.concatenate(rows, axis=0)

    @jax.named_scope("pack")
    def pack(js, f, parts):
        for i in range(SIDE):
            chosen = picks(js, f, i)
            for s in parts:
                cols = slice(fine * s, fine * (s + 1))
                rows = jnp.dot(chosen, line[f, s, i], preferred_element_type=F32).astype(BF)
                for n, j in enumerate(js):
                    for q in range(SIDE):
                        at = SLOTS * (n * SIDE + q)
                        packed[j, f, q, i, :, cols] = rows[at : at + SLOTS, :]
        for j in js:
            for i in range(SIDE):
                for s in parts:
                    cols = slice(fine * s, fine * (s + 1))
                    to = slice(wide * f + fine * s, wide * f + fine * (s + 1))
                    xin[j, 0, block_rows(f, i), to] = packed[j, f, then_at[f], i, :, cols]

    def dispatch(j, f, first, count):
        for k in (1, 3, 2):
            q = lax.rem(then_at[f] + k, SIDE)
            for i in range(SIDE):
                remote(
                    packed.at[j, f, q, i, :, pl.ds(first, count)],
                    xin.at[j, 0, block_rows(f, i), pl.ds(wide * f + first, count)], xs.at[0], xr.at[j],
                    (sec, on_then(f, q))).start()

    for f in range(2):
        await_bytes(slots.at[f, pl.ds(0, SIDE - 1)], nr.at[f])
    for s in range(PARTS):
        for f in range(2):
            with jax.named_scope("line_wait"):
                await_bytes(line.at[f, s, pl.ds(0, SIDE - 1)], lr.at[f, s])
            pack([0], f, [s])
            dispatch(0, f, fine * s, fine)

    def dispatch_all(j):
        for f in range(2):
            dispatch(j, f, 0, wide)

    for f in range(2):
        pack(list(range(1, BATCHES)), f, range(PARTS))
    dispatch_all(1)

    def sib_x(j):
        return remote(xin.at[j, 0], xin.at[j, 1], fs.at[0], fr.at[j], sibling)

    own_rows = pl.ds(pl.multiple_of(hrows * c, hrows), hrows)
    sib_rows = pl.ds(pl.multiple_of(hrows * (1 - c), hrows), hrows)

    def sib_p(j, g):
        return remote(part.at[j, g, sib_rows, :], sib.at[j, g], ps.at[0], pr.at[j, g], sibling)

    def own_sum(j, k, first, count):
        g, i = PLACE[k % NZ]
        cols = slice(chunk * i + first, chunk * i + first + count)
        return part[j, g, own_rows, cols].astype(F32) + sib[j, g, :, cols].astype(F32)

    def sign(u):
        return 1 - 2 * (u % 2)

    def chain_a(u, t, p):
        return remote(asend.at[u, t, p], arecv.at[u, t, p], as_.at[0], ar.at[u, t, p], zdev(-sign(u)))

    def chain_b(u, t, p):
        return remote(bsend.at[u, t, p], brecv.at[u, t, p], bs.at[0], br.at[u, t, p], zdev(sign(u)))

    @jax.named_scope("chain_step")
    def chain_step(u, t):
        j = CHAINS[u]
        ka, kb = 4 + sign(u) * t, 4 - sign(u) * (1 + t)
        if t < 2:
            sib_p(j, t).wait_recv()
        for p in range(PIECES):
            total = own_sum(j, ka, col * p, col)
            if t > 0:
                chain_a(u, t - 1, p).wait_recv()
                total = total + arecv[u, t - 1, p].astype(F32)
            asend[u, t, p] = total.astype(BF)
            chain_a(u, t, p).start()
            if t < 3:
                total = own_sum(j, kb, col * p, col)
                if t > 0:
                    chain_b(u, t - 1, p).wait_recv()
                    total = total + brecv[u, t - 1, p].astype(F32)
                bsend[u, t, p] = total.astype(BF)
                chain_b(u, t, p).start()

    mine = pl.ds(pl.multiple_of(SLOTS * me, SLOTS), SLOTS)

    def give_back(srcs, dst, send_sem, recv_sem):
        for core, src in enumerate(srcs):
            for i in range(blocks):
                b = c * blocks + i
                rows = pl.ds(SLOTS * i, SLOTS)
                own = jnp.logical_and(b == me, c == core)

                @pl.when(jnp.logical_not(own))
                def _():
                    remote(src.at[rows, :], dst.at[mine, :], send_sem, recv_sem, (z * 2 + core, b)).start()

                @pl.when(own)
                def _():
                    dst[mine, :] = src[rows, :]

    home = c == me // blocks

    def await_rows(ref, sem):
        @pl.when(home)
        def _():
            await_bytes(ref.at[pl.ds(0, SLOTS * (experts - 1)), :], sem)

        @pl.when(jnp.logical_not(home))
        def _():
            await_bytes(ref, sem)

    @jax.named_scope("chain_end")
    def chain_end(u):
        for p in range(PIECES):
            chain_a(u, 3, p).wait_recv()
            chain_b(u, 2, p).wait_recv()
            total = own_sum(CHAINS[u], 0, col * p, col) + arecv[u, 3, p].astype(F32) + brecv[u, 2, p].astype(F32)
            ret_out[u, :, col * p : col * (p + 1)] = total.astype(BF)
        give_back([ret_out.at[u]] * 2, ret.at[u], rs.at[CHAINS[u]], rr.at[u])

    @jax.named_scope("late_back")
    def late_back(n):
        j = LATE[n]
        for g in range(2):
            sib_p(j, g).wait_recv()
            for h, (i0, i1) in enumerate(STAGES):
                cols = slice(chunk * i0, chunk * i1)
                total = part[j, g, own_rows, cols].astype(F32) + sib[j, g, :, cols].astype(F32)
                late_out[n, g, :, cols] = total.astype(BF)
        for h, (i0, i1) in enumerate(STAGES):
            cols = pl.ds(chunk * i0, chunk * (i1 - i0))
            give_back(
                [late_out.at[n, g, :, cols] for g in range(2)], late_in.at[n, :, cols], rs.at[j], rl.at[n, h])

    own_toks = pl.ds(pl.multiple_of(htoks * c, htoks), htoks)

    @jax.named_scope("mix")
    def mix(u):
        await_rows(ret.at[u], rr.at[u])
        term = jnp.dot(chi[CHAINS[u]], ret[u], preferred_element_type=F32)
        term = term + jnp.dot(clo[CHAINS[u]], ret[u], preferred_element_type=F32)
        acc[...] = term if u == 0 else acc[...] + term

    def give(p, at, k, first, count, sem):
        here = mixed.at[p, lax.rem(z + at + NZ, NZ), pl.ds(pl.multiple_of(htoks * c, htoks) + first, count), :]
        return remote(here, here, os_.at[0], or_.at[p, sem], zdev(k))

    def pass_on(p):
        for side in (1, -1):
            await_bytes(mixed.at[p, 0, pl.ds(0, htoks), :], or_.at[p, (1 - side) // 2])
            give(p, -2 * side, side, 0, htoks, 2).start()
            give(p, -2 * side, 2 * side, htoks // 4 * (1 - side), htoks // 2, 2).start()

    def hand(p):
        here = mixed.at[p, :, own_toks, :]
        return remote(here, here, gs.at[0], gr.at[p], sibling)

    @jax.named_scope("late_mix")
    def late_mix(h):
        i0, i1 = STAGES[h]
        cols = slice(chunk * i0, chunk * i1)
        term = jnp.zeros((toks, chunk * (i1 - i0)), F32)
        for n, j in enumerate(LATE):
            await_rows(late_in.at[n, :, pl.ds(chunk * i0, chunk * (i1 - i0))], rl.at[n, h])
            term = term + jnp.dot(chi[j], late_in[n, :, cols], preferred_element_type=F32)
            term = term + jnp.dot(clo[j], late_in[n, :, cols], preferred_element_type=F32)
        for i in range(i0, i1):
            zsend[i] = term[:, chunk * (i - i0) : chunk * (i - i0 + 1)].astype(BF)
        low, high = pl.ds(0, htoks), pl.ds(htoks, htoks)

        @pl.when(c == 0)
        def _():
            if h == 0:
                relay_send(zsend.at[0, low, :], 0, pl.ds(toks, htoks), 2)
                relay_send(zsend.at[0, high, :], 1, pl.ds(toks, htoks), -2)
                relay_send(zsend.at[1], 0, pl.ds(0, toks), 1)
                relay_send(zsend.at[2], 1, pl.ds(0, toks), -1)
            else:
                zrecv[0] = zsend[3, :htoks, :]
                remote(zsend.at[3, high, :], zrecv.at[0], zs.at[0], zr.at[0], sibling).start()

        @pl.when(c == 1)
        def _():
            owner_send(2 + h, 1 + h, 1 - 2 * h)

    def relay_send(src, side, rows, k):
        remote(src, relay.at[side, rows, :], zs.at[0], zq.at[0], zdev(k, 1)).start()

    def owner_send(i, n, k):
        for core in range(2):
            remote(zsend.at[i, pl.ds(htoks * core, htoks), :], zrecv.at[n], zs.at[0], zr.at[0], zdev(k, core)).start()

    @jax.named_scope("relay_sum")
    def relay_sum():
        @pl.when(c == 1)
        def _():
            await_bytes(relay, zq.at[0])
            for side in range(2):
                total = zsend[side].astype(F32) + relay[side, :toks, :].astype(F32)
                far = slice(htoks * side, htoks * (side + 1))
                near = slice(htoks * (1 - side), htoks * (2 - side))
                zsend[side, near, :] = total[near, :].astype(BF)
                zsend[side, far, :] = (total[far, :] + relay[side, toks:, :].astype(F32)).astype(BF)
                owner_send(side, 3 + side, 2 - 4 * side)

    def await_parts(ref, sem):
        @pl.when(c == 1)
        def _():
            await_bytes(ref, sem)

        @pl.when(c == 0)
        def _():
            await_bytes(ref.at[pl.ds(0, 4)], sem)

    @jax.named_scope("gather")
    def gather():
        await_parts(zrecv, zr.at[0])
        for p in range(PIECES):
            cols = slice(col * p, col * (p + 1))
            total = acc[own_toks, cols]
            for k in range(5):
                total = total + zrecv[k, :, cols].astype(F32)
            mixed[p, z, own_toks, :] = total.astype(BF)
            for k in (2, -2, 1, -1):
                give(p, 0, k, 0, htoks, {2: 0, -2: 1, 1: 2, -1: 2}[k]).start()

    @jax.named_scope("take")
    def take(j):
        if j >= BATCHES:
            return
        await_bytes(xin.at[j, 0, pl.ds(0, SLOTS * SIDE * (SIDE - 1)), :], xr.at[j])
        if j + 2 < BATCHES:
            dispatch_all(j + 2)
        sib_x(j).start()

    @jax.named_scope("up")
    def up(j, h):
        gate = jnp.dot(xin[j, h], wg[h], preferred_element_type=F32)
        raised = jnp.dot(xin[j, h], wu[h], preferred_element_type=F32)
        if h == 0:
            gacc[...] = gate
            uacc[...] = raised
            return None
        gate = gacc[...] + gate
        raised = uacc[...] + raised
        return (gate / (1.0 + jnp.exp(-gate)) * raised).astype(BF)

    @jax.named_scope("down")
    def down(j, hidden):
        for g in range(2):
            part[j, g] = jnp.dot(hidden, wd[g], preferred_element_type=F32).astype(BF)
            sib_p(j, g).start()
            if j == 0 and g == 0:
                take(1)

    def after(j):
        if j == 0:
            chain_step(0, 0)
        if j == 1:
            late_back(0)
            chain_step(0, 1)
        if j == 2:
            chain_step(1, 0)
        if j == 3:
            chain_step(0, 2)
            chain_step(1, 1)
            late_back(1)

    take(0)
    for j in range(BATCHES):
        if j == 0:
            loads[0].wait()
            loads[1].wait()
        up(j, 0)
        if j != 2:
            after(j - 1)
        if j == 0:
            loads[2].wait()
            loads[3].wait()
        with jax.named_scope("sib_wait"):
            sib_x(j).wait_recv()
        hidden = up(j, 1)
        if j == 2:
            after(1)
        if j == 0:
            await_bytes(wd, w_sem.at[4])
        if j > 0:
            take(j + 1)
        down(j, hidden)
    after(BATCHES - 1)
    chain_step(1, 2)
    chain_step(0, 3)
    chain_step(1, 3)
    late_mix(0)
    chain_end(1)
    chain_end(0)
    late_mix(1)
    relay_sum()
    mix(0)
    mix(1)
    gather()

    with jax.named_scope("drain"):
        await_bytes(slots.at[:, pl.ds(0, SIDE - 1)], ns.at[0])
        await_bytes(line.at[:, :, pl.ds(0, SIDE - 1)], ls.at[0])
        await_bytes(packed.at[:, :, pl.ds(0, SIDE - 1)], xs.at[0])
        await_bytes(xin.at[:, 0], fs.at[0])
        await_bytes(part.at[:, :, pl.ds(0, hrows), :], ps.at[0])
        await_bytes(asend, as_.at[0])
        await_bytes(bsend, bs.at[0])
        for u, j in enumerate(CHAINS):
            await_rows(ret.at[u], rs.at[j])
        for n, j in enumerate(LATE):
            await_rows(late_in.at[n], rs.at[j])
        @pl.when(c == 0)
        def _():
            await_bytes(late_in.at[0, pl.ds(0, 7 * htoks * chunk // half), :], zs.at[0])

        @pl.when(c == 1)
        def _():
            await_bytes(zsend, zs.at[0])

    for p in range(PIECES):
        with jax.named_scope("pass_on"):
            pass_on(p)
    for p in range(PIECES):
        with jax.named_scope("gather_wait"):
            await_bytes(mixed.at[p, pl.ds(0, NZ - 3), pl.ds(0, htoks), :], or_.at[p, 2])
        hand(p).start()
    for p in range(PIECES):
        with jax.named_scope("hand_wait"):
            hand(p).wait_recv()
        for k in range(NZ):
            out[:, chunk * k + col * p : chunk * k + col * (p + 1)] = mixed[p, k]
    await_bytes(mixed.at[:, pl.ds(0, NZ - 1), pl.ds(0, htoks), :], os_.at[0])
    await_bytes(mixed.at[:, :, pl.ds(0, htoks), :], gs.at[0])


def on_device(tokens, norm_gain, expert_ids, gates, gate_proj, up_proj, down_proj):
    toks, features = tokens.shape
    experts = lax.axis_size("expert")
    width = gate_proj.shape[2]
    half, chunk = features // 2, features // NZ
    fine, col = half // (2 * PARTS), chunk // PIECES
    rows = experts * SLOTS
    hrows = rows // 2
    dma = pltpu.SemaphoreType.DMA
    vmem = pl.BlockSpec(memory_space=pltpu.VMEM)
    hbm = pl.BlockSpec(memory_space=pl.ANY)
    b = BATCHES
    scratch = [
        pltpu.VMEM((toks, features), BF),
        pltpu.VMEM((2, half, width), BF),
        pltpu.VMEM((2, half, width), BF),
        pltpu.VMEM((2, width, half), BF),
        pltpu.VMEM((2, PARTS, SIDE, toks, fine), BF),
        pltpu.VMEM((2, SIDE, experts, toks), F32),
        pltpu.VMEM((b, toks, rows), BF),
        pltpu.VMEM((b, toks, rows), BF),
        pltpu.VMEM((b, 2, SIDE, SIDE, SLOTS, half // 2), BF),
        pltpu.VMEM((b, 2, rows, half), BF),
        pltpu.VMEM((rows, width), F32),
        pltpu.VMEM((rows, width), F32),
        pltpu.VMEM((b, 2, rows, half), BF),
        pltpu.VMEM((b, 2, hrows, half), BF),
        pltpu.VMEM((len(CHAINS), 4, PIECES, hrows, col), BF),
        pltpu.VMEM((len(CHAINS), 4, PIECES, hrows, col), BF),
        pltpu.VMEM((len(CHAINS), 3, PIECES, hrows, col), BF),
        pltpu.VMEM((len(CHAINS), 3, PIECES, hrows, col), BF),
        pltpu.VMEM((len(CHAINS), hrows, chunk), BF),
        pltpu.VMEM((len(CHAINS), rows, chunk), BF),
        pltpu.VMEM((len(LATE), 2, hrows, half), BF),
        pltpu.VMEM((len(LATE), rows, half), BF),
        pltpu.VMEM((NZ // 2, toks, chunk), BF),
        pltpu.VMEM((5, toks // 2, chunk), BF),
        pltpu.VMEM((2, toks + toks // 2, chunk), BF),
        pltpu.VMEM((toks, chunk), F32),
        pltpu.VMEM((PIECES, NZ, toks, col), BF),
        dma((6,)),
        dma((1,)), dma((2, PARTS)),
        dma((1,)), dma((2,)),
        dma((1,)), dma((b,)),
        dma((1,)), dma((b,)),
        dma((1,)), dma((b, 2)),
        dma((1,)), dma((len(CHAINS), 4, PIECES)),
        dma((1,)), dma((len(CHAINS), 3, PIECES)),
        dma((b,)), dma((len(CHAINS),)), dma((len(LATE), len(STAGES))),
        dma((1,)), dma((1,)), dma((1,)),
        dma((1,)), dma((PIECES, 3)),
        dma((1,)), dma((PIECES,)),
    ]
    return pl.pallas_call(
        kernel,
        out_shape=pltpu.VMEM((toks, features), BF),
        in_specs=[hbm, vmem, vmem, vmem, hbm, hbm, hbm],
        out_specs=vmem,
        scratch_shapes=scratch,
        compiler_params=pltpu.CompilerParams(
            collective_id=0, has_side_effects=True, vmem_limit_bytes=60 << 20
        ),
    )(tokens, norm_gain.reshape(1, -1), expert_ids.T, gates.T, gate_proj, up_proj, down_proj)


def solution(mesh):
    return jax.shard_map(
        on_device,
        mesh=mesh,
        in_specs=(
            P("expert", None),
            P(),
            P("expert", None),
            P("expert", None),
            P("expert", None, "section"),
            P("expert", None, "section"),
            P("expert", "section", None),
        ),
        out_specs=P("expert", None),
        check_vma=False,
    )
```

```python
import jax
import jax.numpy as jnp
from jax import lax
from jax.experimental import pallas as pl
from jax.experimental.pallas import tpu as pltpu
from jax.sharding import PartitionSpec as P

MESH = pl.DeviceIdType.MESH
BATCHES = 4
CHAINS = (0, 2)
LATE = (1, 3)
SLOTS = 16
NZ = 8
SIDE = 4
XY = [(dx, dy) for dx in range(SIDE) for dy in range(SIDE) if (dx, dy) != (0, 0)]
ORDER = ((4, 3, 5, 0), (2, 6, 1, 7))
STAGES = ((0, 3), (3, 4))
PLACE = {k: (g, i) for g, ks in enumerate(ORDER) for i, k in enumerate(ks)}
PIECES = 3
PARTS = 3
BF = jnp.bfloat16
F32 = jnp.float32


def kernel(
    tok_hbm, gain, ids, gates, wg_hbm, wu_hbm, wd_hbm, out,
    tok, wg, wu, wd, line, slots, chi, clo, packed, xin, gacc, uacc, part, sib,
    asend, arecv, bsend, brecv, ret_out, ret, late_out, late_in, zsend, zrecv, relay, acc, mixed,
    w_sem, ls, lr, ns, nr, xs, xr, fs, fr, ps, pr, as_, ar, bs, br, rs, rr, rl, zs, zr, zq, os_, or_, gs, gr,
):
    sec, me = lax.axis_index("section"), lax.axis_index("expert")
    z, c = sec // 2, sec % 2
    x, y = me // SIDE, me % SIDE
    experts = SIDE * SIDE
    blocks = experts // 2
    toks = tok.shape[0]
    htoks = toks // 2
    fine = line.shape[4]
    wide = fine * PARTS
    half = 2 * wide
    col = mixed.shape[3]
    chunk = col * PIECES
    hrows = blocks * SLOTS
    first_at, then_at = (x, y), (y, x)

    def on_first(f, i):
        return i * SIDE + y if f == 0 else x * SIDE + i

    def on_then(f, q):
        return x * SIDE + q if f == 0 else q * SIDE + y

    def zdev(dz, core=c):
        return (lax.rem(z + dz + 2 * NZ, NZ) * 2 + core, me)

    def xydev(dx, dy):
        return lax.rem(x + dx, SIDE) * SIDE + lax.rem(y + dy, SIDE)

    other = z * 2 + 1 - c
    sibling = (other, me)

    token_load = pltpu.make_async_copy(tok_hbm, tok, w_sem.at[5])
    token_load.start()

    barrier = pltpu.get_barrier_semaphore()
    for dx, dy in XY:
        for s in (sec, other):
            pl.semaphore_signal(barrier, inc=1, device_id=(s, xydev(dx, dy)), device_id_type=MESH)
    pl.semaphore_signal(barrier, inc=1, device_id=sibling, device_id_type=MESH)
    for k in range(1, NZ):
        for core in range(2):
            pl.semaphore_signal(barrier, inc=1, device_id=zdev(k, core), device_id_type=MESH)

    loads = []
    for h in range(2):
        lines = pl.ds(pl.multiple_of(half * lax.rem(c + h, 2), half), half)
        loads.append(pltpu.make_async_copy(wg_hbm.at[0, lines, :], wg.at[h], w_sem.at[2 * h]))
        loads.append(pltpu.make_async_copy(wu_hbm.at[0, lines, :], wu.at[h], w_sem.at[2 * h + 1]))
    for load in loads:
        load.start()
    for k in range(NZ):
        cols = pl.ds(pl.multiple_of(chunk * lax.rem(z + k, NZ), chunk), chunk)
        g, i = PLACE[k]
        pltpu.make_async_copy(wd_hbm.at[0, :, cols], wd.at[g, :, pl.ds(chunk * i, chunk)], w_sem.at[4]).start()

    def await_bytes(ref, sem):
        pltpu.make_async_copy(ref, ref, sem).wait()

    e_iota = lax.broadcasted_iota(jnp.int32, (experts, toks), 0)
    named = jnp.zeros((experts, toks), jnp.bool_)
    weight = jnp.zeros((experts, toks), F32)
    for k in range(ids.shape[0]):
        hit = e_iota == ids[k : k + 1, :]
        named = named | hit
        weight = weight + jnp.where(hit, gates[k : k + 1, :], 0.0)
    earlier = lax.broadcasted_iota(jnp.int32, (toks, toks), 0) < lax.broadcasted_iota(jnp.int32, (toks, toks), 1)
    slot = jnp.dot(
        jnp.where(named, 1.0, 0.0).astype(BF), jnp.where(earlier, 1.0, 0.0).astype(BF), preferred_element_type=F32)
    slot = jnp.where(named, slot, -1.0)
    for f in range(2):
        slots[f, first_at[f]] = slot

    with jax.named_scope("norm"):
        token_load.wait()
        values = tok[...].astype(F32)
        average = jnp.mean(values, axis=-1, keepdims=True)
        centered = values - average
        variance = jnp.mean(centered * centered, axis=-1, keepdims=True)
        scale = lax.rsqrt(variance + 1e-05)
        for f in range(2):
            for s in range(PARTS):
                cols = pl.ds(pl.multiple_of(half * c + wide * f + fine * s, fine), fine)
                part_values = tok[:, cols].astype(F32) - average
                line[f, s, first_at[f]] = (part_values * scale * gain[:, cols]).astype(BF)

    def remote(src, dst, send_sem, recv_sem, to):
        return pltpu.make_async_remote_copy(
            src_ref=src, dst_ref=dst, send_sem=send_sem, recv_sem=recv_sem, device_id=to, device_id_type=MESH)

    with jax.named_scope("entry_wait"):
        pl.semaphore_wait(barrier, 2 * len(XY) + 2 * NZ - 1)
    def mates(f):
        return [(sec, on_first(f, lax.rem(first_at[f] + k, SIDE))) for k in (1, 3, 2)]

    for f in range(2):
        for to in mates(f):
            here = slots.at[f, first_at[f]]
            remote(here, here, ns.at[0], nr.at[f], to).start()
    for s in range(PARTS):
        for f in range(2):
            for to in mates(f):
                here = line.at[f, s, first_at[f]]
                remote(here, here, ls.at[0], lr.at[f, s], to).start()

    def shares(low, count, hi, lo):
        places = lax.broadcasted_iota(jnp.int32, (count, toks), 0).astype(F32) + float(low)
        rows = [jnp.where(slot[e : e + 1, :] == places, weight[e : e + 1, :], 0.0) for e in range(experts)]
        share = jnp.transpose(jnp.concatenate(rows, axis=0))
        top = share.astype(BF)
        hi[...] = top
        lo[...] = (share - top.astype(F32)).astype(BF)

    with jax.named_scope("shares"):
        for j in range(BATCHES):
            shares(SLOTS * j, SLOTS, chi.at[j], clo.at[j])

    def block_rows(f, i):
        return pl.ds(pl.multiple_of(SLOTS * on_first(f, i), SLOTS), SLOTS)

    s_iota = lax.broadcasted_iota(jnp.int32, (SLOTS, toks), 0).astype(F32)

    def picks(js, f, i):
        rows = []
        for j in js:
            for q in range(SIDE):
                row = slots[f, i, pl.ds(on_then(f, q), 1), :]
                rows.append(jnp.where((row - float(SLOTS * j)) == s_iota, 1.0, 0.0).astype(BF))
        return jnp.concatenate(rows, axis=0)

    @jax.named_scope("pack")
    def pack(js, f, parts):
        for i in range(SIDE):
            chosen = picks(js, f, i)
            for s in parts:
                cols = slice(fine * s, fine * (s + 1))
                rows = jnp.dot(chosen, line[f, s, i], preferred_element_type=F32).astype(BF)
                for n, j in enumerate(js):
                    for q in range(SIDE):
                        at = SLOTS * (n * SIDE + q)
                        packed[j, f, q, i, :, cols] = rows[at : at + SLOTS, :]
        for j in js:
            for i in range(SIDE):
                for s in parts:
                    cols = slice(fine * s, fine * (s + 1))
                    to = slice(wide * f + fine * s, wide * f + fine * (s + 1))
                    xin[j, 0, block_rows(f, i), to] = packed[j, f, then_at[f], i, :, cols]

    def dispatch(j, f, first, count):
        for k in (1, 3, 2):
            q = lax.rem(then_at[f] + k, SIDE)
            for i in range(SIDE):
                remote(
                    packed.at[j, f, q, i, :, pl.ds(first, count)],
                    xin.at[j, 0, block_rows(f, i), pl.ds(wide * f + first, count)], xs.at[0], xr.at[j],
                    (sec, on_then(f, q))).start()

    for f in range(2):
        await_bytes(slots.at[f, pl.ds(0, SIDE - 1)], nr.at[f])
    for s in range(PARTS):
        for f in range(2):
            with jax.named_scope("line_wait"):
                await_bytes(line.at[f, s, pl.ds(0, SIDE - 1)], lr.at[f, s])
            pack([0], f, [s])
            dispatch(0, f, fine * s, fine)

    def dispatch_all(j):
        for f in range(2):
            dispatch(j, f, 0, wide)

    for f in range(2):
        pack(list(range(1, BATCHES)), f, range(PARTS))
    dispatch_all(1)

    def sib_x(j):
        return remote(xin.at[j, 0], xin.at[j, 1], fs.at[0], fr.at[j], sibling)

    own_rows = pl.ds(pl.multiple_of(hrows * c, hrows), hrows)
    sib_rows = pl.ds(pl.multiple_of(hrows * (1 - c), hrows), hrows)

    def sib_p(j, g):
        return remote(part.at[j, g, sib_rows, :], sib.at[j, g], ps.at[0], pr.at[j, g], sibling)

    def own_sum(j, k, first, count):
        g, i = PLACE[k % NZ]
        cols = slice(chunk * i + first, chunk * i + first + count)
        return part[j, g, own_rows, cols].astype(F32) + sib[j, g, :, cols].astype(F32)

    def sign(u):
        return 1 - 2 * (u % 2)

    def chain_a(u, t, p):
        return remote(asend.at[u, t, p], arecv.at[u, t, p], as_.at[0], ar.at[u, t, p], zdev(-sign(u)))

    def chain_b(u, t, p):
        return remote(bsend.at[u, t, p], brecv.at[u, t, p], bs.at[0], br.at[u, t, p], zdev(sign(u)))

    @jax.named_scope("chain_step")
    def chain_step(u, t):
        j = CHAINS[u]
        ka, kb = 4 + sign(u) * t, 4 - sign(u) * (1 + t)
        if t < 2:
            sib_p(j, t).wait_recv()
        for p in range(PIECES):
            total = own_sum(j, ka, col * p, col)
            if t > 0:
                chain_a(u, t - 1, p).wait_recv()
                total = total + arecv[u, t - 1, p].astype(F32)
            asend[u, t, p] = total.astype(BF)
            chain_a(u, t, p).start()
            if t < 3:
                total = own_sum(j, kb, col * p, col)
                if t > 0:
                    chain_b(u, t - 1, p).wait_recv()
                    total = total + brecv[u, t - 1, p].astype(F32)
                bsend[u, t, p] = total.astype(BF)
                chain_b(u, t, p).start()

    mine = pl.ds(pl.multiple_of(SLOTS * me, SLOTS), SLOTS)

    def give_back(srcs, dst, send_sem, recv_sem):
        for core, src in enumerate(srcs):
            for i in range(blocks):
                b = c * blocks + i
                rows = pl.ds(SLOTS * i, SLOTS)
                own = jnp.logical_and(b == me, c == core)

                @pl.when(jnp.logical_not(own))
                def _():
                    remote(src.at[rows, :], dst.at[mine, :], send_sem, recv_sem, (z * 2 + core, b)).start()

                @pl.when(own)
                def _():
                    dst[mine, :] = src[rows, :]

    home = c == me // blocks

    def await_rows(ref, sem):
        @pl.when(home)
        def _():
            await_bytes(ref.at[pl.ds(0, SLOTS * (experts - 1)), :], sem)

        @pl.when(jnp.logical_not(home))
        def _():
            await_bytes(ref, sem)

    @jax.named_scope("chain_end")
    def chain_end(u):
        for p in range(PIECES):
            chain_a(u, 3, p).wait_recv()
            chain_b(u, 2, p).wait_recv()
            total = own_sum(CHAINS[u], 0, col * p, col) + arecv[u, 3, p].astype(F32) + brecv[u, 2, p].astype(F32)
            ret_out[u, :, col * p : col * (p + 1)] = total.astype(BF)
        give_back([ret_out.at[u]] * 2, ret.at[u], rs.at[CHAINS[u]], rr.at[u])

    @jax.named_scope("late_back")
    def late_back(n):
        j = LATE[n]
        for g in range(2):
            sib_p(j, g).wait_recv()
            for h, (i0, i1) in enumerate(STAGES):
                cols = slice(chunk * i0, chunk * i1)
                total = part[j, g, own_rows, cols].astype(F32) + sib[j, g, :, cols].astype(F32)
                late_out[n, g, :, cols] = total.astype(BF)
        for h, (i0, i1) in enumerate(STAGES):
            cols = pl.ds(chunk * i0, chunk * (i1 - i0))
            give_back(
                [late_out.at[n, g, :, cols] for g in range(2)], late_in.at[n, :, cols], rs.at[j], rl.at[n, h])

    own_toks = pl.ds(pl.multiple_of(htoks * c, htoks), htoks)

    @jax.named_scope("mix")
    def mix(u):
        await_rows(ret.at[u], rr.at[u])
        term = jnp.dot(chi[CHAINS[u]], ret[u], preferred_element_type=F32)
        term = term + jnp.dot(clo[CHAINS[u]], ret[u], preferred_element_type=F32)
        acc[...] = term if u == 0 else acc[...] + term

    def give(p, at, k, first, count, sem):
        here = mixed.at[p, lax.rem(z + at + NZ, NZ), pl.ds(pl.multiple_of(htoks * c, htoks) + first, count), :]
        return remote(here, here, os_.at[0], or_.at[p, sem], zdev(k))

    def pass_on(p):
        for side in (1, -1):
            await_bytes(mixed.at[p, 0, pl.ds(0, htoks), :], or_.at[p, (1 - side) // 2])
            give(p, -2 * side, side, 0, htoks, 2).start()
            give(p, -2 * side, 2 * side, htoks // 4 * (1 - side), htoks // 2, 2).start()

    def hand(p):
        here = mixed.at[p, :, own_toks, :]
        return remote(here, here, gs.at[0], gr.at[p], sibling)

    @jax.named_scope("late_mix")
    def late_mix(h):
        i0, i1 = STAGES[h]
        cols = slice(chunk * i0, chunk * i1)
        term = jnp.zeros((toks, chunk * (i1 - i0)), F32)
        for n, j in enumerate(LATE):
            await_rows(late_in.at[n, :, pl.ds(chunk * i0, chunk * (i1 - i0))], rl.at[n, h])
            term = term + jnp.dot(chi[j], late_in[n, :, cols], preferred_element_type=F32)
            term = term + jnp.dot(clo[j], late_in[n, :, cols], preferred_element_type=F32)
        for i in range(i0, i1):
            zsend[i] = term[:, chunk * (i - i0) : chunk * (i - i0 + 1)].astype(BF)
        low, high = pl.ds(0, htoks), pl.ds(htoks, htoks)

        @pl.when(c == 0)
        def _():
            if h == 0:
                relay_send(zsend.at[0, low, :], 0, pl.ds(toks, htoks), 2)
                relay_send(zsend.at[0, high, :], 1, pl.ds(toks, htoks), -2)
                relay_send(zsend.at[1], 0, pl.ds(0, toks), 1)
                relay_send(zsend.at[2], 1, pl.ds(0, toks), -1)
            else:
                zrecv[0] = zsend[3, :htoks, :]
                remote(zsend.at[3, high, :], zrecv.at[0], zs.at[0], zr.at[0], sibling).start()

        @pl.when(c == 1)
        def _():
            owner_send(2 + h, 1 + h, 1 - 2 * h)

    def relay_send(src, side, rows, k):
        remote(src, relay.at[side, rows, :], zs.at[0], zq.at[0], zdev(k, 1)).start()

    def owner_send(i, n, k):
        for core in range(2):
            remote(zsend.at[i, pl.ds(htoks * core, htoks), :], zrecv.at[n], zs.at[0], zr.at[0], zdev(k, core)).start()

    @jax.named_scope("relay_sum")
    def relay_sum():
        @pl.when(c == 1)
        def _():
            await_bytes(relay, zq.at[0])
            for side in range(2):
                total = zsend[side].astype(F32) + relay[side, :toks, :].astype(F32)
                far = slice(htoks * side, htoks * (side + 1))
                near = slice(htoks * (1 - side), htoks * (2 - side))
                zsend[side, near, :] = total[near, :].astype(BF)
                zsend[side, far, :] = (total[far, :] + relay[side, toks:, :].astype(F32)).astype(BF)
                owner_send(side, 3 + side, 2 - 4 * side)

    def await_parts(ref, sem):
        @pl.when(c == 1)
        def _():
            await_bytes(ref, sem)

        @pl.when(c == 0)
        def _():
            await_bytes(ref.at[pl.ds(0, 4)], sem)

    @jax.named_scope("gather")
    def gather():
        await_parts(zrecv, zr.at[0])
        for p in range(PIECES):
            cols = slice(col * p, col * (p + 1))
            total = acc[own_toks, cols]
            for k in range(5):
                total = total + zrecv[k, :, cols].astype(F32)
            mixed[p, z, own_toks, :] = total.astype(BF)
            for k in (2, -2, 1, -1):
                give(p, 0, k, 0, htoks, {2: 0, -2: 1, 1: 2, -1: 2}[k]).start()

    @jax.named_scope("take")
    def take(j):
        if j >= BATCHES:
            return
        await_bytes(xin.at[j, 0, pl.ds(0, SLOTS * SIDE * (SIDE - 1)), :], xr.at[j])
        if j + 2 < BATCHES:
            dispatch_all(j + 2)
        sib_x(j).start()

    @jax.named_scope("up")
    def up(j, h):
        gate = jnp.dot(xin[j, h], wg[h], preferred_element_type=F32)
        raised = jnp.dot(xin[j, h], wu[h], preferred_element_type=F32)
        if h == 0:
            gacc[...] = gate
            uacc[...] = raised
            return None
        gate = gacc[...] + gate
        raised = uacc[...] + raised
        return (gate / (1.0 + jnp.exp(-gate)) * raised).astype(BF)

    @jax.named_scope("down")
    def down(j, hidden):
        for g in range(2):
            part[j, g] = jnp.dot(hidden, wd[g], preferred_element_type=F32).astype(BF)
            sib_p(j, g).start()
            if j == 0 and g == 0:
                take(1)

    def after(j):
        if j == 0:
            chain_step(0, 0)
        if j == 1:
            late_back(0)
            chain_step(0, 1)
        if j == 2:
            chain_step(1, 0)
        if j == 3:
            chain_step(0, 2)
            chain_step(1, 1)
            late_back(1)

    take(0)
    for j in range(BATCHES):
        if j == 0:
            loads[0].wait()
            loads[1].wait()
        up(j, 0)
        if j != 2:
            after(j - 1)
        if j == 0:
            loads[2].wait()
            loads[3].wait()
        with jax.named_scope("sib_wait"):
            sib_x(j).wait_recv()
        hidden = up(j, 1)
        if j == 2:
            after(1)
        if j == 0:
            await_bytes(wd, w_sem.at[4])
        if j > 0:
            take(j + 1)
        down(j, hidden)
    after(BATCHES - 1)
    chain_step(0, 3)
    chain_step(1, 2)
    chain_step(1, 3)
    late_mix(0)
    chain_end(1)
    chain_end(0)
    late_mix(1)
    relay_sum()
    mix(0)
    mix(1)
    gather()

    with jax.named_scope("drain"):
        await_bytes(slots.at[:, pl.ds(0, SIDE - 1)], ns.at[0])
        await_bytes(line.at[:, :, pl.ds(0, SIDE - 1)], ls.at[0])
        await_bytes(packed.at[:, :, pl.ds(0, SIDE - 1)], xs.at[0])
        await_bytes(xin.at[:, 0], fs.at[0])
        await_bytes(part.at[:, :, pl.ds(0, hrows), :], ps.at[0])
        await_bytes(asend, as_.at[0])
        await_bytes(bsend, bs.at[0])
        for u, j in enumerate(CHAINS):
            await_rows(ret.at[u], rs.at[j])
        for n, j in enumerate(LATE):
            await_rows(late_in.at[n], rs.at[j])
        @pl.when(c == 0)
        def _():
            await_bytes(late_in.at[0, pl.ds(0, 7 * htoks * chunk // half), :], zs.at[0])

        @pl.when(c == 1)
        def _():
            await_bytes(zsend, zs.at[0])

    for p in range(PIECES):
        with jax.named_scope("pass_on"):
            pass_on(p)
    for p in range(PIECES):
        with jax.named_scope("gather_wait"):
            await_bytes(mixed.at[p, pl.ds(0, NZ - 3), pl.ds(0, htoks), :], or_.at[p, 2])
        hand(p).start()
    for p in range(PIECES):
        with jax.named_scope("hand_wait"):
            hand(p).wait_recv()
        for k in range(NZ):
            out[:, chunk * k + col * p : chunk * k + col * (p + 1)] = mixed[p, k]
    await_bytes(mixed.at[:, pl.ds(0, NZ - 1), pl.ds(0, htoks), :], os_.at[0])
    await_bytes(mixed.at[:, :, pl.ds(0, htoks), :], gs.at[0])


def on_device(tokens, norm_gain, expert_ids, gates, gate_proj, up_proj, down_proj):
    toks, features = tokens.shape
    experts = lax.axis_size("expert")
    width = gate_proj.shape[2]
    half, chunk = features // 2, features // NZ
    fine, col = half // (2 * PARTS), chunk // PIECES
    rows = experts * SLOTS
    hrows = rows // 2
    dma = pltpu.SemaphoreType.DMA
    vmem = pl.BlockSpec(memory_space=pltpu.VMEM)
    hbm = pl.BlockSpec(memory_space=pl.ANY)
    b = BATCHES
    scratch = [
        pltpu.VMEM((toks, features), BF),
        pltpu.VMEM((2, half, width), BF),
        pltpu.VMEM((2, half, width), BF),
        pltpu.VMEM((2, width, half), BF),
        pltpu.VMEM((2, PARTS, SIDE, toks, fine), BF),
        pltpu.VMEM((2, SIDE, experts, toks), F32),
        pltpu.VMEM((b, toks, rows), BF),
        pltpu.VMEM((b, toks, rows), BF),
        pltpu.VMEM((b, 2, SIDE, SIDE, SLOTS, half // 2), BF),
        pltpu.VMEM((b, 2, rows, half), BF),
        pltpu.VMEM((rows, width), F32),
        pltpu.VMEM((rows, width), F32),
        pltpu.VMEM((b, 2, rows, half), BF),
        pltpu.VMEM((b, 2, hrows, half), BF),
        pltpu.VMEM((len(CHAINS), 4, PIECES, hrows, col), BF),
        pltpu.VMEM((len(CHAINS), 4, PIECES, hrows, col), BF),
        pltpu.VMEM((len(CHAINS), 3, PIECES, hrows, col), BF),
        pltpu.VMEM((len(CHAINS), 3, PIECES, hrows, col), BF),
        pltpu.VMEM((len(CHAINS), hrows, chunk), BF),
        pltpu.VMEM((len(CHAINS), rows, chunk), BF),
        pltpu.VMEM((len(LATE), 2, hrows, half), BF),
        pltpu.VMEM((len(LATE), rows, half), BF),
        pltpu.VMEM((NZ // 2, toks, chunk), BF),
        pltpu.VMEM((5, toks // 2, chunk), BF),
        pltpu.VMEM((2, toks + toks // 2, chunk), BF),
        pltpu.VMEM((toks, chunk), F32),
        pltpu.VMEM((PIECES, NZ, toks, col), BF),
        dma((6,)),
        dma((1,)), dma((2, PARTS)),
        dma((1,)), dma((2,)),
        dma((1,)), dma((b,)),
        dma((1,)), dma((b,)),
        dma((1,)), dma((b, 2)),
        dma((1,)), dma((len(CHAINS), 4, PIECES)),
        dma((1,)), dma((len(CHAINS), 3, PIECES)),
        dma((b,)), dma((len(CHAINS),)), dma((len(LATE), len(STAGES))),
        dma((1,)), dma((1,)), dma((1,)),
        dma((1,)), dma((PIECES, 3)),
        dma((1,)), dma((PIECES,)),
    ]
    return pl.pallas_call(
        kernel,
        out_shape=pltpu.VMEM((toks, features), BF),
        in_specs=[hbm, vmem, vmem, vmem, hbm, hbm, hbm],
        out_specs=vmem,
        scratch_shapes=scratch,
        compiler_params=pltpu.CompilerParams(
            collective_id=0, has_side_effects=True, vmem_limit_bytes=60 << 20
        ),
    )(tokens, norm_gain.reshape(1, -1), expert_ids.T, gates.T, gate_proj, up_proj, down_proj)


def solution(mesh):
    return jax.shard_map(
        on_device,
        mesh=mesh,
        in_specs=(
            P("expert", None),
            P(),
            P("expert", None),
            P("expert", None),
            P("expert", None, "section"),
            P("expert", None, "section"),
            P("expert", "section", None),
        ),
        out_specs=P("expert", None),
        check_vma=False,
    )
```
